128 devices in a mesh: dp: 32 (over x, y_lo, z), tensor: 4 (over y_hi, core).
Axes of the slice: x: 4, y: 4 (y_hi: 2, y_lo: 2; y = y_hi * 2 + y_lo), z: 4, core: 2. Of those that a mesh axis runs over, the one named last changes fastest.
Arguments:
- context: bfloat16 [4096, 6144], P('dp', 'tensor'), may hold values from -6 to 6
- out_weight: bfloat16 [6144, 12288], P('tensor', 'dp'), may hold values from -0.078125 to 0.078125
- grad_out: bfloat16 [4096, 12288], P('tensor', 'dp'), may hold values from -6 to 6
Outputs:
- grad_context: bfloat16 [4096, 6144], P('dp', 'tensor')
- grad_weight: float32 [6144, 12288], P('tensor', 'dp')
The draws below stay inside these ranges and needn't reach their ends.
All inputs are finite; a program needn't handle non-finite values.
Results may differ from the reference program's by a relative error of at most 0.001.
Values may be sent and summed in bfloat16 or wider, within the bound.
A program may use at most 128 MiB of HBM per device.

```python
import jax
import jax.numpy as jnp
from jax import lax

D = 12288
HID = 6144
TOKENS = 4096


def with_spikes(drawn, own_key, source, target, shards_of, factor):
    owner, partner = [(jnp.arange(drawn.shape[axis_at]) // (drawn.shape[axis_at] // shards_of)).reshape([-1 if axis == axis_at else 1 for axis in range(drawn.ndim)]) for axis_at in (source, target)]
    chosen = jax.random.permutation(own_key, shards_of)[partner]
    strong = (owner == chosen) | (owner == (partner + shards_of // 2) % shards_of)
    return jnp.where(strong, factor * drawn, drawn)


def level_of(own_key, extent, shards, least, largest):
    def one(position, shards_of):
        heights = jax.random.uniform(jax.random.fold_in(jax.random.fold_in(own_key, 6), position), (shards_of,), jnp.float32, least / len(shards), largest / len(shards))
        return jnp.repeat(jnp.exp(heights), extent[position] // shards_of).reshape((-1,) + (1,) * (len(extent) - position - 1))

    level = one(*shards[0])
    for cut in shards[1:]:
        level = level * one(*cut)
    return level


def normal_values(own_key, shape, width, reach, split=(), dtype=jnp.bfloat16):
    gain = level_of(own_key, shape, split, -0.22, 0.18) if split else 1.0
    entries = jax.random.normal(own_key, shape, jnp.float32) * width * gain
    return jnp.minimum(jnp.maximum(entries, -reach), reach).astype(dtype)


def bell_draw_with(rng, shape, deviation, reach, cuts, heavy, kind=jnp.bfloat16):
    drawn = deviation * jax.random.normal(rng, shape, jnp.float32)
    if cuts:
        drawn = drawn * level_of(rng, shape, cuts, -0.22, 0.18)
    return jnp.clip(with_spikes(drawn, jax.random.fold_in(rng, 3), *heavy), -reach, reach).astype(kind)


def setup_inputs(seed: int = 0) -> dict:
    key_of = jax.random.split(jax.random.key(seed), 4)
    return {
        "context": normal_values(key_of[0], (TOKENS, HID), 1.0, 6.0, ((0, 32), (1, 4))),
        "out_weight": normal_values(key_of[1], (HID, D), HID ** -0.5, 0.078125, ((0, 4), (1, 32))),
        "grad_out": bell_draw_with(key_of[2], (TOKENS, D), 1.0, 6.0, ((0, 4), (1, 32)), (1, 0, 32, 2.75)),
    }


def reference(context, out_weight, grad_out):
    grad_context = lax.dot_general(grad_out, out_weight, (((1,), (1,)), ((), ())), preferred_element_type=jnp.float32).astype(jnp.bfloat16)
    summed = lax.dot_general(context, grad_out, (((0,), (0,)), ((), ())), preferred_element_type=jnp.float32)
    grad_weight = summed * (float(TOKENS) ** -0.5)
    return grad_context, grad_weight.astype(jnp.float32)
```

```python
import functools

import jax
import jax.numpy as jnp
from jax import lax
from jax.experimental import pallas as pl
from jax.experimental.pallas import tpu as pltpu
from jax.sharding import Mesh
from jax.sharding import PartitionSpec as P

AXES = ("x", "ylo", "z", "yhi", "core")
BF16 = jnp.bfloat16
F32 = jnp.float32
N_SEMS = 240
PIECES = 4
ORDER = (
    "ca D", "g0 ownZ", "g0 ownY", "g0 ownC", "c0", "locals", "locals done", "g0 ownT", "g1 ownY", "ca Y",
    "c fown", "c x- own", "c x+ own", "c D", "g0 C", "c x+ fown", "c x- fown", "g0 Y", "c fD", "ca Z", "g0 Z",
    "g1 ownZ", "c last own", "c x- D", "in0 Y", "g0 ZC0", "g0 YC1", "c x+ D", "c x- fD", "g1 Y", "g0 YZ1",
    "g0 ZC1", "c last fown", "w Z", "w D", "w Y", "c Y", "g2 ownT", "c Z", "c x+ fD", "g0 YC0", "g1 ownC",
    "g1 YC1", "g0 YZC1", "c fY", "in0 own", "c last D", "c x- Y", "g3 ownT", "g1 Z", "g0 YZ0", "c fZ", "c x- Z",
    "c x+ Y", "g2 ownY", "g1 YZ1", "in0 D", "g1 C", "g3 ownC", "c x- fY", "c x+ Z", "g1 ownT", "in1 Y",
    "g1 ZC1", "g2 ownC", "g2 ownZ", "c last fD", "c last Y", "g0 YZC0", "c x- fZ", "c x+ fY", "in0 Z",
    "g1 YZC1", "c last Z", "turn 2", "turn 3", "c x+ fZ", "c last fY", "g3 C", "c last fZ", "turn 0", "turn 1",
    "g1 YZ0", "w in", "sums 0", "early 0", "g2 C", "g1 ZC0", "g2 Y", "g1 YZC0", "in1 D", "g2 Z", "g3 ownZ",
    "in2 Y", "g1 YC0", "g3 ownY", "in1 Z", "g2 YC1", "g3 YC0", "g3 ZC0", "in1 own", "sums 1", "g2 ZC1",
    "early 1", "g2 ZC0", "g2 YC0", "g2 YZ1", "g2 YZ0", "in2 own", "in2 D", "r L 1", "r R 1", "g2 YZC1", "g3 Z",
    "g3 Y", "g2 YZC0", "in3 Y", "in2 Z", "sums 2", "f 1", "g3 YZ0", "g3 YZ1", "g3 ZC1", "f 2", "early 2",
    "in3 D", "late D", "r 1", "late Y", "g3 YC1", "g3 YZC0", "in3 own", "late own", "g3 YZC1", "f 3", "r L 2",
    "in3 Z", "sums 3", "late Z", "r R 2", "r R 3", "f 0", "r L 3", "r 2", "r 3", "gc out", "end",
)


class Links:
    def __init__(self, send, recv, anyone):
        self.send, self.recv, self.anyone = send, recv, anyone
        self.index, self.started = {}, {}

    def slot(self, name):
        return self.index.setdefault(name, len(self.index))

    def start(self, name, src, dst, device):
        i = self.slot(name)
        copy = pltpu.make_async_remote_copy(
            src_ref=src, dst_ref=dst, send_sem=self.send.at[i], recv_sem=self.recv.at[i],
            device_id=device, device_id_type=pl.DeviceIdType.MESH,
        )
        copy.start()
        self.started[name] = src

    def wait(self, name, dst):
        i = self.slot(name)
        pltpu.make_async_remote_copy(
            src_ref=dst, dst_ref=dst, send_sem=self.send.at[i], recv_sem=self.recv.at[i],
            device_id=self.anyone, device_id_type=pl.DeviceIdType.MESH,
        ).wait_recv()

    def drain(self):
        for name, sent in self.started.items():
            i = self.index[name]
            pltpu.make_async_remote_copy(
                src_ref=sent, dst_ref=sent, send_sem=self.send.at[i], recv_sem=self.recv.at[i],
                device_id=self.anyone, device_id_type=pl.DeviceIdType.MESH,
            ).wait_send()


def run_tasks(tasks, net):
    assert len(ORDER) == len(tasks)
    for name in ORDER:
        waits, body, _ = tasks[name]
        for what, where in waits:
            net.wait(what, where)
        body()


def kernel(factor, c_ref, w_ref, g_ref, gc_ref, gw_ref, cg, ct, gg, wb, part, r1, r2, qz, fz, gw2, gcs, send, recv, local):
    x, p, z, q, core = (lax.axis_index(a) for a in AXES)
    o = 1 - p
    z_near = z + 1 - 2 * lax.rem(z, 2)
    z_far = 3 - z
    zd = lax.rem(lax.div(z + 1, 2), 2)
    zg = lax.div(z, 2)

    x_up, x_down = (lax.rem(x + 1, 4), p, z, q, core), (lax.rem(x + 3, 4), p, z, q, core)
    dev = {
        "Y": (x, o, z, q, core),
        "Z": (x, p, z_near, q, core),
        "D": (x, o, z_near, q, core),
        "C": (x, o, z, 1 - q, core),
        "T": (x, p, z, q, 1 - core),
        "F": (x, p, z_far, q, core),
    }
    barrier = pltpu.get_barrier_semaphore()
    everyone = (x_up, x_down, *dev.values())
    for other in everyone:
        pl.semaphore_signal(barrier, inc=1, device_id=other, device_id_type=pl.DeviceIdType.MESH)
    pl.semaphore_wait(barrier, len(everyone))

    net = Links(send, recv, dev["T"])
    xs = [lax.rem(x + d, 4) for d in range(4)]
    slot = {"own": 2 * p + zd, "Y": 2 * o + zd, "Z": 2 * p + 1 - zd, "D": 2 * o + 1 - zd}
    home = {"own": (p, z), "Y": (o, z), "Z": (p, z_near), "D": (o, z_near)}
    far = {b: (pp, 3 - zz) for b, (pp, zz) in home.items()}

    def span(b):
        return pl.ds(pl.multiple_of(384 * slot[b], 128), 384)

    k_own, k_cross = 2 * q + core, 2 * (1 - q) + core
    k_twin, k_far = 2 * q + 1 - core, 2 * (1 - q) + 1 - core
    zc = [2 * (1 - zg), 2 * (1 - zg) + 1, 2 * zg, 2 * zg + 1]

    tasks = {}

    def task(name, waits=(), after=()):
        def add(body):
            tasks[name] = (tuple(waits), body, tuple(after))
            return body

        return add

    def c_to(b):
        @task(f"ca {b}")
        def _():
            net.start(("ca", b), c_ref.at[:, span(b)], cg.at[x, p, z], dev[b])

    for b in ("D", "Y", "Z"):
        c_to(b)

    @task("c0")
    def _():
        mine = c_ref.at[:, span("own")]
        net.start(("cz", "own"), mine, cg.at[x, p, z], dev["F"])
        for name, device in (("x+", x_up), ("x-", x_down)):
            net.start(("cx", name, "own"), mine, cg.at[x, p, z], device)

    copies = [
        pltpu.make_async_copy(c_ref.at[:, span("own")], cg.at[x, p, z], local.at[0]),
        pltpu.make_async_copy(g_ref, gg.at[slot["own"], k_own], local.at[1]),
        pltpu.make_async_copy(w_ref.at[span("own")], wb.at[slot["own"]], local.at[2]),
    ]

    @task("locals")
    def _():
        for copy in copies:
            copy.start()

    @task("locals done", after=("locals",))
    def _():
        for copy in copies:
            copy.wait()

    place = {**home, **{f"f{b}": at for b, at in far.items()}}

    def c_round(b):
        block = cg.at[(x, *place[b])]
        for name, device in (("x+", x_up), ("x-", x_down)):
            net.start(("cx", name, b), block, block, device)

    def c_gather(b):
        block = cg.at[(x, *place[b])]

        @task(f"c {b}", waits=[(("ca", b), block)], after=("c0", f"ca {b}"))
        def _():
            net.start(("cz", b), block, block, dev["F"])
            c_round(b)

    def c_across(b):
        @task(f"c f{b}", waits=[(("cz", b), cg.at[(x, *far[b])])], after=("c0",) if b == "own" else (f"c {b}",))
        def _():
            c_round(f"f{b}")

    def c_pass(name, b):
        dx, device = (3, x_up) if name == "x+" else (1, x_down)
        block, last = cg.at[(xs[dx], *place[b])], cg.at[(xs[2], *place[b])]
        on = (b[-1] in "nD") == (name == "x+")

        @task(f"c {name} {b}", waits=[(("cx", name, b), block)], after=("c0",) if b == "own" else (f"c {b}",))
        def _():
            if on:
                net.start(("cf", b), block, block, device)

        if on:

            @task(f"c last {b}", waits=[(("cf", b), last)], after=(f"c {name} {b}",))
            def _():
                pass

    for b in ("Y", "Z", "D"):
        c_gather(b)
    for b in home:
        c_across(b)
    for b in place:
        c_pass("x+", b)
        c_pass("x-", b)

    def turned(j):
        ct[j] = cg[:, :, zc[j]].reshape(1024, 384).T

    for pre in ("", "f"):
        names = [f"c {n} {pre}{b}" for n in ("x+", "x-", "last") for b in home]
        names += [f"c {pre}{b}" for b in home if pre + b != "own"]
        for j in (2, 3) if pre == "" else (0, 1):

            @task(f"turn {j}", after=(*names, "locals done"))
            def _(j=j):
                turned(j)

    def w_to(b):
        @task(f"w {b}")
        def _():
            net.start(("w", b), w_ref.at[span(b)], wb.at[slot["own"]], dev[b])

    for b in ("D", "Y", "Z"):
        w_to(b)

    def round_x(j, d):
        zz = zc[j]
        if d == 2:
            net.start(("r1 L", j), part.at[xs[2], 0, zz], r1.at[j, 0], x_down)
            net.start(("r1 R", j), part.at[xs[2], 1, zz], r1.at[j, 1], x_up)
        elif d == 3:
            net.start(("r2 +", j, 1), part.at[xs[3], 1, zz], r2.at[j, 0, 1], x_down)
        elif d == 1:
            net.start(("r2 -", j, 0), part.at[xs[1], 0, zz], r2.at[j, 1, 0], x_up)

    def g_tasks(j):
        zz = zc[j]
        both = slice(None)

        def at(b, k, pp):
            return gg.at[slot[b], k, pp, zz]

        def fwd(to, b, k, pp):
            net.start(("g", j, to, b, k, pp if isinstance(pp, int) else 2), at(b, K[k], pp), at(b, K[k], pp), dev[to])

        K = {"h": k_own, "c": k_cross}
        H = {"h": k_twin, "c": k_far}

        heard = {b: [] for b in home}
        here = {b: [] for b in home}

        def own_to(to):
            @task(f"g{j} own{to}")
            def _():
                net.start(("g", j, to, "own", "h", 2), g_ref.at[:, zz], gg.at[slot["own"], k_own, :, zz], dev[to])

        for to in ("C", "Y", "Z", "T"):
            own_to(to)

        heard["own"].append((("g", j, "T", "own", "h", 2), at("own", k_twin, both)))

        def got(name, to, sent, b, k, pp, sends):
            heard[b].append((("g", j, "T", b, k, pp if isinstance(pp, int) else 2), at(b, H[k], pp)))
            here[b].append(f"g{j} {name}")
            key = ("g", j, to, *sent, pp if isinstance(pp, int) else 2)

            @task(f"g{j} {name}", waits=[(key, at(b, K[k], pp))], after=(f"g{j} own{to}",))
            def _():
                for dest, part_p in sends:
                    fwd(dest, b, k, part_p)
                fwd("T", b, k, pp)

        got("Y", "Y", ("own", "h"), "Y", "h", both, (("C", 1), ("Z", 1)))
        got("Z", "Z", ("own", "h"), "Z", "h", both, (("C", 1), ("Y", 0)))
        got("C", "C", ("own", "h"), "Y", "c", both, (("Y", 0), ("Z", 0)))
        got("YZ0", "Y", ("Z", "h"), "D", "h", 0, (("C", 0),))
        got("YZ1", "Z", ("Y", "h"), "D", "h", 1, (("C", 1),))
        got("YC0", "Y", ("Y", "c"), "own", "c", 0, ())
        got("YC1", "C", ("Y", "h"), "own", "c", 1, ())
        got("ZC0", "Z", ("Y", "c"), "D", "c", 0, ())
        got("ZC1", "C", ("Z", "h"), "D", "c", 1, ())
        got("YZC0", "C", ("D", "h"), "Z", "c", 0, ())
        got("YZC1", "C", ("D", "h"), "Z", "c", 1, ())
        def slot_in(b):
            @task(f"in{j} {b}", waits=heard[b], after=(*here[b], f"g{j} ownT", "locals done"))
            def _():
                pass

        for b in home:
            slot_in(b)
        if j == 0:

            @task("w in", waits=[(("w", b), wb.at[slot[b]]) for b in ("D", "Y", "Z")], after=("w D", "w Y", "w Z", "locals done"))
            def _():
                pass

        @task(f"sums {j}", after=("w in", *(f"in{j} {b}" for b in home)))
        def _():
            weight = jnp.concatenate([wb[s] for s in range(4)], axis=1)
            for k in range(4):
                r = jnp.concatenate([gg[s, k, :, zz].reshape(256, 384) for s in range(4)], axis=1)
                t = lax.dot_general(r, weight, (((1,), (1,)), ((), ())), preferred_element_type=F32)
                part[k, :, zz] = t.reshape(2, 128, 384)
            if j == 0:
                for d in (2, 1, 3, 0):
                    net.start(("fz", d), part.at[xs[d], :, zz], fz.at[d], dev["F"])
            elif j != 2:
                for d in (2, 1, 3):
                    round_x(j, d)

    for j in range(4):
        g_tasks(j)

    def across(d):
        zz = zc[2]

        @task(f"f {d}", waits=[(("fz", d), fz.at[d])], after=("sums 0", "sums 2"))
        def _():
            part[xs[d], :, zz] = part[xs[d], :, zz] + fz[d]
            round_x(2, d)

    for d in (2, 1, 3, 0):
        across(d)

    near = lax.rem(z, 2)

    def gc_mine():
        return pltpu.make_async_copy(gcs.at[near, p], gc_ref.at[:, span("own")], local.at[3])

    def reduce_tasks(j):
        zz = zc[j]
        ready = {3: "f 3", 1: "f 1", 0: "f 0"} if j == 2 else dict.fromkeys((3, 1, 0), f"sums {j}")

        @task(f"r L {j}", waits=[(("r1 L", j), r1.at[j, 0])], after=(ready[3],))
        def _():
            part[xs[3], 0, zz] = part[xs[3], 0, zz] + r1[j, 0]
            net.start(("r2 +", j, 0), part.at[xs[3], 0, zz], r2.at[j, 0, 0], x_down)

        @task(f"r R {j}", waits=[(("r1 R", j), r1.at[j, 1])], after=(ready[1],))
        def _():
            part[xs[1], 1, zz] = part[xs[1], 1, zz] + r1[j, 1]
            net.start(("r2 -", j, 1), part.at[xs[1], 1, zz], r2.at[j, 1, 1], x_up)

        waits = [((f"r2 {s}", j, pp), r2.at[j, i, pp]) for i, s in enumerate("+-") for pp in range(2)]
        if j == 3:
            waits.append(("qz", qz))

        @task(f"r {j}", waits=waits, after=(f"r L {j}", f"r R {j}", ready[0], *(("r 1",) if j == 3 else ())))
        def _():
            total = part[x, :, zz] + r2[j, 0] + r2[j, 1]
            if j == 1:
                part[x, :, zz] = total
                net.start("qz", part.at[x, :, zz], qz, dev["F"])
                return
            gcs[j - 2] = (total if j == 2 else total + qz[...]).astype(BF16)

    for j in (1, 2, 3):
        reduce_tasks(j)

    @task("gc out", after=("r 2", "r 3"))
    def _():
        net.start(("gc", "D"), gcs.at[1 - near, o], gc_ref.at[:, span("own")], dev["D"])
        net.start(("gc", "Y"), gcs.at[near, o], gc_ref.at[:, span("own")], dev["Y"])
        net.start(("gc", "Z"), gcs.at[1 - near, p], gc_ref.at[:, span("own")], dev["Z"])
        gc_mine().start()

    def products(s, js):
        total = 0.0
        for j in js:
            rhs = gg[s, :, :, zc[j]].reshape(1024, 384)
            total = total + jnp.dot(ct[j], rhs, preferred_element_type=F32)
        return total

    slots = ("Y", "D", "own", "Z")

    def early(j):
        @task(f"early {j}", after=(f"sums {j}", f"turn {j}", *((f"early {j - 1}",) if j else ())))
        def _():
            for s in range(4):
                t = products(s, (j,))
                gw2[s] = gw2[s] + t if j else t

    for j in range(3):
        early(j)

    gw_copy = pltpu.make_async_copy(gw2.at[slot["own"]], gw_ref.at[span("own")], local.at[4])

    def late(b):
        @task(f"late {b}", after=("early 2", "turn 3", f"in3 {b}"))
        def _():
            s = slot[b]
            gw2[s] = (gw2[s] + products(s, (3,))) * factor
            if b == "own":
                gw_copy.start()
            else:
                net.start(("gw", b), gw2.at[s], gw_ref.at[span("own")], dev[b])

    for b in slots:
        late(b)

    @task(
        "end",
        waits=[(("gw", b), gw_ref.at[span(b)]) for b in ("Y", "Z", "D")]
        + [(("gc", b), gc_ref.at[:, span(b)]) for b in ("Y", "Z", "D")],
        after=("gc out", *(f"late {b}" for b in slots)),
    )
    def _():
        gw_copy.wait()
        gc_mine().wait()

    run_tasks(tasks, net)
    net.drain()
    assert len(net.index) <= N_SEMS


def hand_over(gc_ref, gw_ref, gc_out, gw_out, gc_buf, gw_buf, read, written):
    rows = gw_ref.shape[0] // PIECES
    routes = [(gw_ref.at[pl.ds(i * rows, rows)], gw_buf.at[pl.ds(i * rows, rows)], gw_out.at[pl.ds(i * rows, rows)]) for i in range(PIECES)]
    routes.append((gc_ref, gc_buf, gc_out))
    reads = [pltpu.make_async_copy(a, b, read.at[i]) for i, (a, b, _) in enumerate(routes)]
    writes = [pltpu.make_async_copy(b, c, written.at[i]) for i, (_, b, c) in enumerate(routes)]
    for copy in reads:
        copy.start()
    for r, w in zip(reads, writes):
        r.wait()
        w.start()
    for copy in writes:
        copy.wait()


SCRATCH = (
    ((4, 2, 4, 128, 384), BF16),
    ((4, 384, 1024), BF16),
    ((4, 4, 2, 4, 128, 384), BF16),
    ((4, 384, 384), BF16),
    ((4, 2, 4, 128, 384), F32),
    ((4, 2, 128, 384), F32),
    ((4, 2, 2, 128, 384), F32),
    ((2, 128, 384), F32),
    ((4, 2, 128, 384), F32),
    ((4, 384, 384), F32),
    ((2, 2, 128, 384), BF16),
)


def on_device(context, out_weight, grad_out):
    factor = float(4096) ** (-0.5)
    anywhere = pl.BlockSpec(memory_space=pl.ANY)
    results = pl.pallas_call(
        functools.partial(kernel, factor),
        out_shape=(
            jax.ShapeDtypeStruct((128, 1536), BF16),
            jax.ShapeDtypeStruct((1536, 384), F32),
        ),
        in_specs=[anywhere] * 3,
        out_specs=(anywhere, anywhere),
        scratch_shapes=[
            *(pltpu.VMEM(shape, dtype) for shape, dtype in SCRATCH),
            pltpu.SemaphoreType.DMA((N_SEMS,)),
            pltpu.SemaphoreType.DMA((N_SEMS,)),
            pltpu.SemaphoreType.DMA((5,)),
        ],
        compiler_params=pltpu.CompilerParams(
            collective_id=0, has_side_effects=True, vmem_limit_bytes=60 * 2**20
        ),
        cost_estimate=pl.CostEstimate(flops=9663676416, bytes_accessed=5111808, transcendentals=0),
        name="both_gradients",
    )(context, out_weight, grad_out.reshape(2, 4, 128, 384))
    return pl.pallas_call(
        hand_over,
        out_shape=tuple(jax.ShapeDtypeStruct(r.shape, r.dtype) for r in results),
        in_specs=[anywhere] * 2,
        out_specs=(anywhere, anywhere),
        scratch_shapes=[
            pltpu.VMEM((128, 1536), BF16),
            pltpu.VMEM((1536, 384), F32),
            pltpu.SemaphoreType.DMA((1 + PIECES,)),
            pltpu.SemaphoreType.DMA((1 + PIECES,)),
        ],
        cost_estimate=pl.CostEstimate(flops=0, bytes_accessed=5505024, transcendentals=0),
        name="hand_over",
    )(*results)


def solution(mesh):
    fine = Mesh(mesh.devices.reshape(4, 2, 4, 2, 2), AXES)
    dp, tensor = ("x", "ylo", "z"), ("yhi", "core")
    return jax.shard_map(
        on_device,
        mesh=fine,
        in_specs=(P(dp, tensor), P(tensor, dp), P(tensor, dp)),
        out_specs=(P(dp, tensor), P(tensor, dp)),
        check_vma=False,
    )
```

```python
import functools

import jax
import jax.numpy as jnp
from jax import lax
from jax.experimental import pallas as pl
from jax.experimental.pallas import tpu as pltpu
from jax.sharding import Mesh
from jax.sharding import PartitionSpec as P

AXES = ("x", "ylo", "z", "yhi", "core")
BF16 = jnp.bfloat16
F32 = jnp.float32
N_SEMS = 240
PIECES = 4
ORDER = (
    1, 2, 0, 3, 69, 70, 71, 44, 68, 45, 4, 5, 117, 6, 7, 15, 9, 46, 13, 50, 8, 10, 16, 17, 72, 73, 74, 11, 20,
    19, 47, 84, 12, 27, 25, 48, 49, 41, 78, 14, 24, 60, 53, 55, 42, 80, 22, 29, 75, 76, 54, 28, 18, 59, 77, 79,
    56, 43, 32, 31, 83, 86, 51, 52, 116, 81, 34, 21, 114, 62, 82, 26, 36, 115, 85, 57, 23, 30, 38, 37, 58, 35,
    33, 39, 151, 152, 61, 154, 153, 40, 158, 156, 157, 120, 155, 91, 63, 66, 64, 90, 87, 89, 65, 88, 67, 118,
    119, 92, 93, 130, 97, 123, 125, 141, 122, 124, 121, 142, 129, 126, 132, 96, 95, 128, 102, 100, 127, 131,
    133, 135, 98, 99, 103, 143, 94, 107, 159, 136, 109, 160, 164, 101, 163, 134, 106, 161, 165, 104, 147, 148,
    105, 108, 111, 112, 110, 137, 113, 139, 162, 138, 166, 144, 145, 140, 146, 149, 150, 167,
)


class Links:
    def __init__(self, send, recv, anyone):
        self.send, self.recv, self.anyone = send, recv, anyone
        self.index, self.started = {}, {}

    def slot(self, name):
        return self.index.setdefault(name, len(self.index))

    def start(self, name, src, dst, device):
        i = self.slot(name)
        copy = pltpu.make_async_remote_copy(
            src_ref=src, dst_ref=dst, send_sem=self.send.at[i], recv_sem=self.recv.at[i],
            device_id=device, device_id_type=pl.DeviceIdType.MESH,
        )
        copy.start()
        self.started[name] = src

    def wait(self, name, dst):
        i = self.slot(name)
        pltpu.make_async_remote_copy(
            src_ref=dst, dst_ref=dst, send_sem=self.send.at[i], recv_sem=self.recv.at[i],
            device_id=self.anyone, device_id_type=pl.DeviceIdType.MESH,
        ).wait_recv()

    def drain(self):
        for name, sent in self.started.items():
            i = self.index[name]
            pltpu.make_async_remote_copy(
                src_ref=sent, dst_ref=sent, send_sem=self.send.at[i], recv_sem=self.recv.at[i],
                device_id=self.anyone, device_id_type=pl.DeviceIdType.MESH,
            ).wait_send()


def run_tasks(tasks, net):
    assert len(ORDER) == len(tasks)
    listed = list(tasks.values())
    for i in ORDER:
        waits, body, _ = listed[i]
        for what, where in waits:
            net.wait(what, where)
        body()


def kernel(factor, c_ref, w_ref, g_ref, gc_ref, gw_ref, cg, ct, gg, wb, part, r1, r2, qz, fz, gw2, gcs, send, recv, local):
    x, p, z, q, core = (lax.axis_index(a) for a in AXES)
    o = 1 - p
    z_near = z + 1 - 2 * lax.rem(z, 2)
    z_far = 3 - z
    zd = lax.rem(lax.div(z + 1, 2), 2)
    zg = lax.div(z, 2)

    x_up, x_down = (lax.rem(x + 1, 4), p, z, q, core), (lax.rem(x + 3, 4), p, z, q, core)
    dev = {
        "Y": (x, o, z, q, core),
        "Z": (x, p, z_near, q, core),
        "D": (x, o, z_near, q, core),
        "C": (x, o, z, 1 - q, core),
        "T": (x, p, z, q, 1 - core),
        "F": (x, p, z_far, q, core),
    }
    barrier = pltpu.get_barrier_semaphore()
    everyone = (x_up, x_down, *dev.values())
    for other in everyone:
        pl.semaphore_signal(barrier, inc=1, device_id=other, device_id_type=pl.DeviceIdType.MESH)
    pl.semaphore_wait(barrier, len(everyone))

    net = Links(send, recv, dev["T"])
    xs = [lax.rem(x + d, 4) for d in range(4)]
    slot = {"own": 2 * p + zd, "Y": 2 * o + zd, "Z": 2 * p + 1 - zd, "D": 2 * o + 1 - zd}
    home = {"own": (p, z), "Y": (o, z), "Z": (p, z_near), "D": (o, z_near)}
    far = {b: (pp, 3 - zz) for b, (pp, zz) in home.items()}

    def span(b):
        return pl.ds(pl.multiple_of(384 * slot[b], 128), 384)

    k_own, k_cross = 2 * q + core, 2 * (1 - q) + core
    k_twin, k_far = 2 * q + 1 - core, 2 * (1 - q) + 1 - core
    zc = [2 * (1 - zg), 2 * (1 - zg) + 1, 2 * zg, 2 * zg + 1]

    tasks = {}

    def task(name, waits=(), after=()):
        def add(body):
            tasks[name] = (tuple(waits), body, tuple(after))
            return body

        return add

    def c_to(b):
        @task(f"ca {b}")
        def _():
            net.start(("ca", b), c_ref.at[:, span(b)], cg.at[x, p, z], dev[b])

    for b in ("D", "Y", "Z"):
        c_to(b)

    @task("c0")
    def _():
        mine = c_ref.at[:, span("own")]
        net.start(("cz", "own"), mine, cg.at[x, p, z], dev["F"])
        for name, device in (("x+", x_up), ("x-", x_down)):
            net.start(("cx", name, "own"), mine, cg.at[x, p, z], device)

    copies = [
        pltpu.make_async_copy(c_ref.at[:, span("own")], cg.at[x, p, z], local.at[0]),
        pltpu.make_async_copy(g_ref, gg.at[slot["own"], k_own], local.at[1]),
        pltpu.make_async_copy(w_ref.at[span("own")], wb.at[slot["own"]], local.at[2]),
    ]

    @task("locals")
    def _():
        for copy in copies:
            copy.start()

    @task("locals done", after=("locals",))
    def _():
        for copy in copies:
            copy.wait()

    place = {**home, **{f"f{b}": at for b, at in far.items()}}

    def c_round(b):
        block = cg.at[(x, *place[b])]
        for name, device in (("x+", x_up), ("x-", x_down)):
            net.start(("cx", name, b), block, block, device)

    def c_gather(b):
        block = cg.at[(x, *place[b])]

        @task(f"c {b}", waits=[(("ca", b), block)], after=("c0", f"ca {b}"))
        def _():
            net.start(("cz", b), block, block, dev["F"])
            c_round(b)

    def c_across(b):
        @task(f"c f{b}", waits=[(("cz", b), cg.at[(x, *far[b])])], after=("c0",) if b == "own" else (f"c {b}",))
        def _():
            c_round(f"f{b}")

    def c_pass(name, b):
        dx, device = (3, x_up) if name == "x+" else (1, x_down)
        block, last = cg.at[(xs[dx], *place[b])], cg.at[(xs[2], *place[b])]
        on = (b[-1] in "nD") == (name == "x+")

        @task(f"c {name} {b}", waits=[(("cx", name, b), block)], after=("c0",) if b == "own" else (f"c {b}",))
        def _():
            if on:
                net.start(("cf", b), block, block, device)

        if on:

            @task(f"c last {b}", waits=[(("cf", b), last)], after=(f"c {name} {b}",))
            def _():
                pass

    for b in ("Y", "Z", "D"):
        c_gather(b)
    for b in home:
        c_across(b)
    for b in place:
        c_pass("x+", b)
        c_pass("x-", b)

    def turned(j):
        ct[j] = cg[:, :, zc[j]].reshape(1024, 384).T

    for pre in ("", "f"):
        names = [f"c {n} {pre}{b}" for n in ("x+", "x-", "last") for b in home]
        names += [f"c {pre}{b}" for b in home if pre + b != "own"]
        for j in (2, 3) if pre == "" else (0, 1):

            @task(f"turn {j}", after=(*names, "locals done"))
            def _(j=j):
                turned(j)

    def w_to(b):
        @task(f"w {b}")
        def _():
            net.start(("w", b), w_ref.at[span(b)], wb.at[slot["own"]], dev[b])

    for b in ("D", "Y", "Z"):
        w_to(b)

    def round_x(j, d):
        zz = zc[j]
        if d == 2:
            net.start(("r1 L", j), part.at[xs[2], 0, zz], r1.at[j, 0], x_down)
            net.start(("r1 R", j), part.at[xs[2], 1, zz], r1.at[j, 1], x_up)
        elif d == 3:
            net.start(("r2 +", j, 1), part.at[xs[3], 1, zz], r2.at[j, 0, 1], x_down)
        elif d == 1:
            net.start(("r2 -", j, 0), part.at[xs[1], 0, zz], r2.at[j, 1, 0], x_up)

    def g_tasks(j):
        zz = zc[j]
        both = slice(None)

        def at(b, k, pp):
            return gg.at[slot[b], k, pp, zz]

        def fwd(to, b, k, pp):
            net.start(("g", j, to, b, k, pp if isinstance(pp, int) else 2), at(b, K[k], pp), at(b, K[k], pp), dev[to])

        K = {"h": k_own, "c": k_cross}
        H = {"h": k_twin, "c": k_far}

        heard = {b: [] for b in home}
        here = {b: [] for b in home}

        def own_to(to):
            @task(f"g{j} own{to}")
            def _():
                net.start(("g", j, to, "own", "h", 2), g_ref.at[:, zz], gg.at[slot["own"], k_own, :, zz], dev[to])

        for to in ("C", "Y", "Z", "T"):
            own_to(to)

        heard["own"].append((("g", j, "T", "own", "h", 2), at("own", k_twin, both)))

        def got(name, to, sent, b, k, pp, sends):
            heard[b].append((("g", j, "T", b, k, pp if isinstance(pp, int) else 2), at(b, H[k], pp)))
            here[b].append(f"g{j} {name}")
            key = ("g", j, to, *sent, pp if isinstance(pp, int) else 2)

            @task(f"g{j} {name}", waits=[(key, at(b, K[k], pp))], after=(f"g{j} own{to}",))
            def _():
                for dest, part_p in sends:
                    fwd(dest, b, k, part_p)
                fwd("T", b, k, pp)

        got("Y", "Y", ("own", "h"), "Y", "h", both, (("C", 1), ("Z", 1)))
        got("Z", "Z", ("own", "h"), "Z", "h", both, (("C", 1), ("Y", 0)))
        got("C", "C", ("own", "h"), "Y", "c", both, (("Y", 0), ("Z", 0)))
        got("YZ0", "Y", ("Z", "h"), "D", "h", 0, (("C", 0),))
        got("YZ1", "Z", ("Y", "h"), "D", "h", 1, (("C", 1),))
        got("YC0", "Y", ("Y", "c"), "own", "c", 0, ())
        got("YC1", "C", ("Y", "h"), "own", "c", 1, ())
        got("ZC0", "Z", ("Y", "c"), "D", "c", 0, ())
        got("ZC1", "C", ("Z", "h"), "D", "c", 1, ())
        got("YZC0", "C", ("D", "h"), "Z", "c", 0, ())
        got("YZC1", "C", ("D", "h"), "Z", "c", 1, ())
        def slot_in(b):
            @task(f"in{j} {b}", waits=heard[b], after=(*here[b], f"g{j} ownT", "locals done"))
            def _():
                pass

        for b in home:
            slot_in(b)
        if j == 0:

            @task("w in", waits=[(("w", b), wb.at[slot[b]]) for b in ("D", "Y", "Z")], after=("w D", "w Y", "w Z", "locals done"))
            def _():
                pass

        def sums(d):
            @task(f"s{j} {d}", after=("w in", *(f"in{j} {b}" for b in home)))
            def _():
                weight = jnp.concatenate([wb[s] for s in range(4)], axis=1)
                r = jnp.concatenate([gg[s, xs[d], :, zz].reshape(256, 384) for s in range(4)], axis=1)
                t = lax.dot_general(r, weight, (((1,), (1,)), ((), ())), preferred_element_type=F32)
                part[xs[d], :, zz] = t.reshape(2, 128, 384)
                if j == 0:
                    net.start(("fz", d), part.at[xs[d], :, zz], fz.at[d], dev["F"])
                elif j != 2:
                    round_x(j, d)

        for d in (2, 1, 3, 0):
            sums(d)

    for j in range(4):
        g_tasks(j)

    def across(d):
        zz = zc[2]

        @task(f"f {d}", waits=[(("fz", d), fz.at[d])], after=("s0 0", f"s2 {d}"))
        def _():
            part[xs[d], :, zz] = part[xs[d], :, zz] + fz[d]
            round_x(2, d)

    for d in (2, 1, 3, 0):
        across(d)

    near = lax.rem(z, 2)

    def gc_mine():
        return pltpu.make_async_copy(gcs.at[near, p], gc_ref.at[:, span("own")], local.at[3])

    def reduce_tasks(j):
        zz = zc[j]
        ready = {3: "f 3", 1: "f 1", 0: "f 0"} if j == 2 else {d: f"s{j} {d}" for d in (3, 1, 0)}

        @task(f"r L {j}", waits=[(("r1 L", j), r1.at[j, 0])], after=(ready[3],))
        def _():
            part[xs[3], 0, zz] = part[xs[3], 0, zz] + r1[j, 0]
            net.start(("r2 +", j, 0), part.at[xs[3], 0, zz], r2.at[j, 0, 0], x_down)

        @task(f"r R {j}", waits=[(("r1 R", j), r1.at[j, 1])], after=(ready[1],))
        def _():
            part[xs[1], 1, zz] = part[xs[1], 1, zz] + r1[j, 1]
            net.start(("r2 -", j, 1), part.at[xs[1], 1, zz], r2.at[j, 1, 1], x_up)

        waits = [((f"r2 {s}", j, pp), r2.at[j, i, pp]) for i, s in enumerate("+-") for pp in range(2)]
        if j == 3:
            waits.append(("qz", qz))

        @task(f"r {j}", waits=waits, after=(f"r L {j}", f"r R {j}", ready[0], *(("r 1",) if j == 3 else ())))
        def _():
            total = part[x, :, zz] + r2[j, 0] + r2[j, 1]
            if j == 1:
                part[x, :, zz] = total
                net.start("qz", part.at[x, :, zz], qz, dev["F"])
                return
            gcs[j - 2] = (total if j == 2 else total + qz[...]).astype(BF16)

    for j in (1, 2, 3):
        reduce_tasks(j)

    @task("gc out", after=("r 2", "r 3"))
    def _():
        net.start(("gc", "D"), gcs.at[1 - near, o], gc_ref.at[:, span("own")], dev["D"])
        net.start(("gc", "Y"), gcs.at[near, o], gc_ref.at[:, span("own")], dev["Y"])
        net.start(("gc", "Z"), gcs.at[1 - near, p], gc_ref.at[:, span("own")], dev["Z"])
        gc_mine().start()

    def products(s, js):
        total = 0.0
        for j in js:
            rhs = gg[s, :, :, zc[j]].reshape(1024, 384)
            total = total + jnp.dot(ct[j], rhs, preferred_element_type=F32)
        return total

    slots = ("Y", "D", "own", "Z")

    def early(j, b):
        @task(f"e{j} {b}", after=(f"in{j} {b}", f"turn {j}", *((f"e{j - 1} {b}",) if j else ())))
        def _():
            s = slot[b]
            t = products(s, (j,))
            gw2[s] = gw2[s] + t if j else t

    for j in range(3):
        for b in slots:
            early(j, b)

    gw_copy = pltpu.make_async_copy(gw2.at[slot["own"]], gw_ref.at[span("own")], local.at[4])

    def late(b):
        @task(f"late {b}", after=(f"e2 {b}", "turn 3", f"in3 {b}"))
        def _():
            s = slot[b]
            gw2[s] = (gw2[s] + products(s, (3,))) * factor
            if b == "own":
                gw_copy.start()
            else:
                net.start(("gw", b), gw2.at[s], gw_ref.at[span("own")], dev[b])

    for b in slots:
        late(b)

    @task(
        "end",
        waits=[(("gw", b), gw_ref.at[span(b)]) for b in ("Y", "Z", "D")]
        + [(("gc", b), gc_ref.at[:, span(b)]) for b in ("Y", "Z", "D")],
        after=("gc out", *(f"late {b}" for b in slots)),
    )
    def _():
        gw_copy.wait()
        gc_mine().wait()

    run_tasks(tasks, net)
    net.drain()
    assert len(net.index) <= N_SEMS


def hand_over(gc_ref, gw_ref, gc_out, gw_out, gc_buf, gw_buf, read, written):
    rows = gw_ref.shape[0] // PIECES
    routes = [(gw_ref.at[pl.ds(i * rows, rows)], gw_buf.at[pl.ds(i * rows, rows)], gw_out.at[pl.ds(i * rows, rows)]) for i in range(PIECES)]
    routes.append((gc_ref, gc_buf, gc_out))
    reads = [pltpu.make_async_copy(a, b, read.at[i]) for i, (a, b, _) in enumerate(routes)]
    writes = [pltpu.make_async_copy(b, c, written.at[i]) for i, (_, b, c) in enumerate(routes)]
    for copy in reads:
        copy.start()
    for r, w in zip(reads, writes):
        r.wait()
        w.start()
    for copy in writes:
        copy.wait()


SCRATCH = (
    ((4, 2, 4, 128, 384), BF16),
    ((4, 384, 1024), BF16),
    ((4, 4, 2, 4, 128, 384), BF16),
    ((4, 384, 384), BF16),
    ((4, 2, 4, 128, 384), F32),
    ((4, 2, 128, 384), F32),
    ((4, 2, 2, 128, 384), F32),
    ((2, 128, 384), F32),
    ((4, 2, 128, 384), F32),
    ((4, 384, 384), F32),
    ((2, 2, 128, 384), BF16),
)


def on_device(context, out_weight, grad_out):
    factor = float(4096) ** (-0.5)
    anywhere = pl.BlockSpec(memory_space=pl.ANY)
    results = pl.pallas_call(
        functools.partial(kernel, factor),
        out_shape=(
            jax.ShapeDtypeStruct((128, 1536), BF16),
            jax.ShapeDtypeStruct((1536, 384), F32),
        ),
        in_specs=[anywhere] * 3,
        out_specs=(anywhere, anywhere),
        scratch_shapes=[
            *(pltpu.VMEM(shape, dtype) for shape, dtype in SCRATCH),
            pltpu.SemaphoreType.DMA((N_SEMS,)),
            pltpu.SemaphoreType.DMA((N_SEMS,)),
            pltpu.SemaphoreType.DMA((5,)),
        ],
        compiler_params=pltpu.CompilerParams(
            collective_id=0, has_side_effects=True, vmem_limit_bytes=60 * 2**20
        ),
        cost_estimate=pl.CostEstimate(flops=9663676416, bytes_accessed=5111808, transcendentals=0),
        name="both_gradients",
    )(context, out_weight, grad_out.reshape(2, 4, 128, 384))
    return pl.pallas_call(
        hand_over,
        out_shape=tuple(jax.ShapeDtypeStruct(r.shape, r.dtype) for r in results),
        in_specs=[anywhere] * 2,
        out_specs=(anywhere, anywhere),
        scratch_shapes=[
            pltpu.VMEM((128, 1536), BF16),
            pltpu.VMEM((1536, 384), F32),
            pltpu.SemaphoreType.DMA((1 + PIECES,)),
            pltpu.SemaphoreType.DMA((1 + PIECES,)),
        ],
        cost_estimate=pl.CostEstimate(flops=0, bytes_accessed=5505024, transcendentals=0),
        name="hand_over",
    )(*results)


def solution(mesh):
    fine = Mesh(mesh.devices.reshape(4, 2, 4, 2, 2), AXES)
    dp, tensor = ("x", "ylo", "z"), ("yhi", "core")
    return jax.shard_map(
        on_device,
        mesh=fine,
        in_specs=(P(dp, tensor), P(tensor, dp), P(tensor, dp)),
        out_specs=(P(dp, tensor), P(tensor, dp)),
        check_vma=False,
    )
```

```python
import functools

import jax
import jax.numpy as jnp
from jax import lax
from jax.experimental import pallas as pl
from jax.experimental.pallas import tpu as pltpu
from jax.sharding import Mesh
from jax.sharding import PartitionSpec as P

AXES = ("x", "ylo", "z", "yhi", "core")
BF16 = jnp.bfloat16
F32 = jnp.float32
N_SEMS = 240
PIECES = 4
HALF = (slice(0, 64), slice(64, 128))
X_FIRST = ("own", "Y")
MAIN, EXTRA = slice(0, 384), slice(384, 512)
ORDER = (
    4, 0, 1, 45, 44, 94, 2, 46, 117, 5, 114, 68, 3, 8, 19, 69, 70, 7, 6, 48, 53, 11, 71, 54, 72, 77, 23, 17, 41,
    42, 18, 51, 55, 43, 56, 50, 74, 22, 78, 28, 79, 47, 116, 20, 57, 24, 31, 30, 93, 49, 73, 115, 59, 25, 62,
    75, 34, 21, 60, 84, 13, 124, 32, 58, 92, 26, 36, 52, 12, 35, 14, 61, 76, 27, 91, 63, 66, 82, 16, 9, 80, 85,
    65, 81, 15, 33, 86, 83, 10, 87, 40, 39, 157, 118, 158, 29, 64, 123, 159, 88, 89, 162, 126, 120, 119, 100,
    101, 121, 90, 129, 95, 141, 142, 161, 127, 125, 38, 128, 132, 122, 102, 156, 107, 130, 104, 143, 131, 133,
    98, 160, 96, 134, 37, 109, 97, 165, 135, 169, 136, 103, 67, 164, 105, 99, 144, 150, 151, 163, 108, 106, 110,
    112, 167, 168, 137, 111, 113, 171, 166, 139, 170, 138, 146, 145, 140, 147, 148, 152, 153, 154, 149, 155,
    172, 173,
)
LATE_ROUTE = (3,)


class Links:
    def __init__(self, send, recv, anyone):
        self.send, self.recv, self.anyone = send, recv, anyone
        self.index, self.started = {}, {}

    def slot(self, name):
        return self.index.setdefault(name, len(self.index))

    def start(self, name, src, dst, device):
        i = self.slot(name)
        copy = pltpu.make_async_remote_copy(
            src_ref=src, dst_ref=dst, send_sem=self.send.at[i], recv_sem=self.recv.at[i],
            device_id=device, device_id_type=pl.DeviceIdType.MESH,
        )
        copy.start()
        self.started[name] = src

    def wait(self, name, dst):
        i = self.slot(name)
        pltpu.make_async_remote_copy(
            src_ref=dst, dst_ref=dst, send_sem=self.send.at[i], recv_sem=self.recv.at[i],
            device_id=self.anyone, device_id_type=pl.DeviceIdType.MESH,
        ).wait_recv()

    def drain(self, later=()):
        for name in [n for n in self.started if n[0] not in later]:
            i, sent = self.index[name], self.started.pop(name)
            pltpu.make_async_remote_copy(
                src_ref=sent, dst_ref=sent, send_sem=self.send.at[i], recv_sem=self.recv.at[i],
                device_id=self.anyone, device_id_type=pl.DeviceIdType.MESH,
            ).wait_send()


def run_tasks(tasks, net):
    assert len(ORDER) == len(tasks)
    listed = list(tasks.values())
    for i in ORDER:
        waits, body, _ = listed[i]
        for what, where in waits:
            net.wait(what, where)
        body()


def kernel(factor, c_ref, w_ref, g_ref, gc_ref, gw_ref, cg, ct, gg, wb, part, r1, r2, qz, fz, gw2, gcs, send, recv, local):
    x, p, z, q, core = (lax.axis_index(a) for a in AXES)
    o = 1 - p
    z_near = z + 1 - 2 * lax.rem(z, 2)
    z_far = 3 - z
    zd = lax.rem(lax.div(z + 1, 2), 2)
    zg = lax.div(z, 2)

    x_up, x_down = (lax.rem(x + 1, 4), p, z, q, core), (lax.rem(x + 3, 4), p, z, q, core)
    dev = {
        "Y": (x, o, z, q, core),
        "Z": (x, p, z_near, q, core),
        "D": (x, o, z_near, q, core),
        "C": (x, o, z, 1 - q, core),
        "T": (x, p, z, q, 1 - core),
        "F": (x, p, z_far, q, core),
    }
    barrier = pltpu.get_barrier_semaphore()
    everyone = (x_up, x_down, *dev.values())
    for other in everyone:
        pl.semaphore_signal(barrier, inc=1, device_id=other, device_id_type=pl.DeviceIdType.MESH)
    pl.semaphore_wait(barrier, len(everyone))

    net = Links(send, recv, dev["T"])
    xs = [lax.rem(x + d, 4) for d in range(4)]
    slot = {"own": 2 * p + zd, "Y": 2 * o + zd, "Z": 2 * p + 1 - zd, "D": 2 * o + 1 - zd}
    home = {"own": (p, z), "Y": (o, z), "Z": (p, z_near), "D": (o, z_near)}
    far = {b: (pp, 3 - zz) for b, (pp, zz) in home.items()}

    opposite = {"own": "D", "Y": "Z", "Z": "Y", "D": "own"}

    def third(b):
        return pl.ds(pl.multiple_of(384 * slot[b], 128), 128)

    def rest(b):
        return pl.ds(pl.multiple_of(384 * slot[b] + 128, 128), 256)

    def span(b):
        return pl.ds(pl.multiple_of(384 * slot[b], 128), 384)

    k_own, k_cross = 2 * q + core, 2 * (1 - q) + core
    k_twin, k_far = 2 * q + 1 - core, 2 * (1 - q) + 1 - core
    zc = [2 * (1 - zg), 2 * (1 - zg) + 1, 2 * zg, 2 * zg + 1]

    tasks = {}

    def task(name, waits=(), after=()):
        def add(body):
            tasks[name] = (tuple(waits), body, tuple(after))
            return body

        return add

    def c_to(b):
        @task(f"ca {b}")
        def _():
            net.start(("ca", b), c_ref.at[:, span(b)], cg.at[x, p, z, :, MAIN], dev[b])
            net.start(("cb", b), c_ref.at[:, third(opposite[b])], cg.at[x, p, z, :, EXTRA], dev[b])

    for b in ("D", "Y", "Z"):
        c_to(b)

    @task("c0", after=("locals done",))
    def _():
        mine = cg.at[x, p, z]
        net.start(("cz", 0, "own"), mine, mine, dev["F"])
        for name, device in (("x+", x_up), ("x-", x_down)):
            net.start(("cx", name, "own"), mine, mine, device)

    copies = [
        pltpu.make_async_copy(c_ref.at[:, span("own")], cg.at[x, p, z, :, MAIN], local.at[0]),
        pltpu.make_async_copy(c_ref.at[:, third("D")], cg.at[x, p, z, :, EXTRA], local.at[5]),
        pltpu.make_async_copy(g_ref, gg.at[slot["own"], k_own], local.at[1]),
        pltpu.make_async_copy(w_ref.at[span("own")], wb.at[slot["own"]], local.at[2]),
    ]

    @task("locals")
    def _():
        for copy in copies:
            copy.start()

    @task("locals done", after=("locals",))
    def _():
        for copy in copies:
            copy.wait()

    place = {**home, **{f"f{b}": at for b, at in far.items()}}

    def c_round(b):
        block = cg.at[(x, *place[b])]
        for name, device in (("x+", x_up), ("x-", x_down)):
            net.start(("cx", name, b), block, block, device)

    def c_gather(b):
        block = cg.at[(x, *place[b])]

        waits = [(("ca", b), cg.at[(x, *place[b], slice(None), MAIN)]), (("cb", b), cg.at[(x, *place[b], slice(None), EXTRA)])]

        @task(f"c {b}", waits=waits, after=("c0", f"ca {b}"))
        def _():
            net.start(("cz", 0, b), block, block, dev["F"])
            c_round(b)

    def c_across(b):
        @task(f"c f{b}", waits=[(("cz", 0, b), cg.at[(x, *far[b])])], after=("c0",) if b == "own" else (f"c {b}",))
        def _():
            if b not in X_FIRST:
                c_round(f"f{b}")

        def from_far(dx, after):
            @task(f"c f{b}{dx}", waits=[(("cz", dx, b), cg.at[(xs[dx], *far[b])])], after=(after,))
            def _():
                pass

        if b in X_FIRST:
            for dx, after in ((1, f"c x- {b}"), (3, f"c x+ {b}"), (2, f"c last {b}")):
                from_far(dx, after)

    def c_pass(name, b):
        dx, device = (3, x_up) if name == "x+" else (1, x_down)
        block, last = cg.at[(xs[dx], *place[b])], cg.at[(xs[2], *place[b])]
        on = (b[-1] in "nD") == (name == "x+")

        @task(f"c {name} {b}", waits=[(("cx", name, b), block)], after=("c0",) if b == "own" else (f"c {b}",))
        def _():
            if on:
                net.start(("cf", b), block, block, device)
            if b in X_FIRST:
                net.start(("cz", dx, b), block, block, dev["F"])

        if on:

            @task(f"c last {b}", waits=[(("cf", b), last)], after=(f"c {name} {b}",))
            def _():
                if b in X_FIRST:
                    net.start(("cz", 2, b), last, last, dev["F"])

    for b in ("Y", "Z", "D"):
        c_gather(b)
    for b in home:
        c_across(b)
    rounds = [b for b in place if b[1:] not in X_FIRST]
    for b in rounds:
        c_pass("x+", b)
        c_pass("x-", b)

    def turned(j):
        ct[j] = cg[:, :, zc[j]].reshape(1024, 512).T

    for pre in ("", "f"):
        names = [f"c {n} {pre}{b}" for n in ("x+", "x-", "last") for b in home if pre + b in rounds]
        names += [f"c {pre}{b}" for b in home if pre + b != "own"]
        names += [f"c f{b}{dx}" for b in X_FIRST for dx in (1, 2, 3) if pre]
        for j in (2, 3) if pre == "" else (0, 1):

            @task(f"turn {j}", after=(*names, "locals done"))
            def _(j=j):
                turned(j)

    def w_to(b):
        @task(f"w {b}")
        def _():
            net.start(("w", b), w_ref.at[span(b)], wb.at[slot["own"]], dev[b])

    for b in ("D", "Y", "Z"):
        w_to(b)

    def round_x(j, d):
        zz = zc[j]
        if d == 2:
            net.start(("r1 L", j), part.at[xs[2], 0, zz], r1.at[j, 0], x_down)
            net.start(("r1 R", j), part.at[xs[2], 1, zz], r1.at[j, 1], x_up)
        elif d == 3:
            net.start(("r2 +", j, 1), part.at[xs[3], 1, zz], r2.at[j, 0, 1], x_down)
        elif d == 1:
            net.start(("r2 -", j, 0), part.at[xs[1], 0, zz], r2.at[j, 1, 0], x_up)

    def g_tasks(j):
        zz = zc[j]
        both = slice(None)

        def at(b, k, pp):
            return gg.at[slot[b], k, pp, zz]

        def fwd(to, b, k, pp):
            net.start(("g", j, to, b, k, pp if isinstance(pp, int) else 2), at(b, K[k], pp), at(b, K[k], pp), dev[to])

        K = {"h": k_own, "c": k_cross}
        H = {"h": k_twin, "c": k_far}

        heard = {b: [] for b in home}
        here = {b: [] for b in home}

        def own_to(to):
            @task(f"g{j} own{to}")
            def _():
                net.start(("g", j, to, "own", "h", 2), g_ref.at[:, zz], gg.at[slot["own"], k_own, :, zz], dev[to])

        for to in ("C", "Y", "Z", "T"):
            own_to(to)

        heard["own"].append((("g", j, "T", "own", "h", 2), at("own", k_twin, both)))

        def got(name, to, sent, b, k, pp, sends):
            heard[b].append((("g", j, "T", b, k, pp if isinstance(pp, int) else 2), at(b, H[k], pp)))
            here[b].append(f"g{j} {name}")
            key = ("g", j, to, *sent, pp if isinstance(pp, int) else 2)

            @task(f"g{j} {name}", waits=[(key, at(b, K[k], pp))], after=(f"g{j} own{to}",))
            def _():
                for dest, part_p in sends:
                    fwd(dest, b, k, part_p)
                fwd("T", b, k, pp)

        late_route = j in LATE_ROUTE
        got("Y", "Y", ("own", "h"), "Y", "h", both, (("C", 1), ("Z", 1)))
        got("YZ1", "Z", ("Y", "h"), "D", "h", 1, (("C", 1),))
        got("YC1", "C", ("Y", "h"), "own", "c", 1, ())
        got("ZC1", "C", ("Z", "h"), "D", "c", 1, ())
        got("YZC1", "C", ("D", "h"), "Z", "c", 1, ())
        if late_route:
            got("Z", "Z", ("own", "h"), "Z", "h", both, (("C", 1), ("Y", 0), ("C", 0)))
            got("C", "C", ("own", "h"), "Y", "c", both, (("Y", 0),))
            got("YZ0", "Y", ("Z", "h"), "D", "h", 0, ())
            got("YC0", "Y", ("Y", "c"), "own", "c", 0, (("Z", 0),))
            got("ZC0", "C", ("Z", "h"), "D", "c", 0, ())
            got("YZC0", "Z", ("own", "c"), "Z", "c", 0, ())
        else:
            got("Z", "Z", ("own", "h"), "Z", "h", both, (("C", 1), ("Y", 0)))
            got("C", "C", ("own", "h"), "Y", "c", both, (("Y", 0), ("Z", 0)))
            got("YZ0", "Y", ("Z", "h"), "D", "h", 0, (("C", 0),))
            got("YC0", "Y", ("Y", "c"), "own", "c", 0, ())
            got("ZC0", "Z", ("Y", "c"), "D", "c", 0, ())
            got("YZC0", "C", ("D", "h"), "Z", "c", 0, ())

        def slot_in(b):
            @task(f"in{j} {b}", waits=heard[b], after=(*here[b], f"g{j} ownT", "locals done"))
            def _():
                pass

        for b in home:
            slot_in(b)
        if j == 0:

            @task("w in", waits=[(("w", b), wb.at[slot[b]]) for b in ("D", "Y", "Z")], after=("w D", "w Y", "w Z", "locals done"))
            def _():
                pass

        def sums(d):
            @task(f"s{j} {d}", after=("w in", *(f"in{j} {b}" for b in home)))
            def _():
                weight = jnp.concatenate([wb[s] for s in range(4)], axis=1)
                r = jnp.concatenate([gg[s, xs[d], :, zz].reshape(256, 384) for s in range(4)], axis=1)
                t = lax.dot_general(r, weight, (((1,), (1,)), ((), ())), preferred_element_type=F32)
                part[xs[d], :, zz] = t.reshape(2, 128, 384)
                if j == 0:
                    net.start(("fz", d), part.at[xs[d], :, zz], fz.at[d], dev["F"])
                elif j != 2:
                    round_x(j, d)

        for d in (2, 1, 3, 0):
            sums(d)

    for j in range(4):
        g_tasks(j)

    def across(d):
        zz = zc[2]

        @task(f"f {d}", waits=[(("fz", d), fz.at[d])], after=("s0 0", f"s2 {d}"))
        def _():
            part[xs[d], :, zz] = part[xs[d], :, zz] + fz[d]
            round_x(2, d)

    for d in (2, 1, 3, 0):
        across(d)

    near = lax.rem(z, 2)

    def gc_mine():
        return pltpu.make_async_copy(gcs.at[near, p], gc_ref.at[:, span("own")], local.at[3])

    def reduce_tasks(j):
        zz = zc[j]
        ready = {3: "f 3", 1: "f 1", 0: "f 0"} if j == 2 else {d: f"s{j} {d}" for d in (3, 1, 0)}
        pieces = HALF if j == 2 else (slice(0, 128),)

        @task(f"r L {j}", waits=[(("r1 L", j), r1.at[j, 0])], after=(ready[3],))
        def _():
            part[xs[3], 0, zz] = part[xs[3], 0, zz] + r1[j, 0]
            for h, rows in enumerate(pieces):
                net.start(("r2 +", j, 0, h), part.at[xs[3], 0, zz, rows], r2.at[j, 0, 0, rows], x_down)

        @task(f"r R {j}", waits=[(("r1 R", j), r1.at[j, 1])], after=(ready[1],))
        def _():
            part[xs[1], 1, zz] = part[xs[1], 1, zz] + r1[j, 1]
            for h, rows in enumerate(pieces):
                net.start(("r2 -", j, 1, h), part.at[xs[1], 1, zz, rows], r2.at[j, 1, 1, rows], x_up)

        waits = [(("r2 +", j, 1), r2.at[j, 0, 1]), (("r2 -", j, 0), r2.at[j, 1, 0])]
        if j == 3:
            waits.append((("qz", 0), qz))

        @task(f"r {j} d", waits=waits, after=(ready[0], *(("r 1 0",) if j == 3 else ())))
        def _():
            pass

        def total(h, rows):
            waits = [(("r2 +", j, 0, h), r2.at[j, 0, 0, rows]), (("r2 -", j, 1, h), r2.at[j, 1, 1, rows])]

            @task(f"r {j} {h}", waits=waits, after=(f"r L {j}", f"r R {j}", f"r {j} d"))
            def _():
                t = part[x, :, zz, rows] + r2[j, 0, :, rows] + r2[j, 1, :, rows]
                if j == 1:
                    part[x, :, zz, rows] = t
                    net.start(("qz", 0), part.at[x, :, zz], qz, dev["F"])
                else:
                    gcs[j - 2, :, rows] = (t if j == 2 else t + qz[:, rows]).astype(BF16)

        for h, rows in enumerate(pieces):
            total(h, rows)

    for j in (1, 2, 3):
        reduce_tasks(j)

    def gc_out(h):
        rows = HALF[h]

        @task(f"gc {h}", after=(f"r 2 {h}", "r 3 0", *(("gc 0",) if h else ())))
        def _():
            to = gc_ref.at[rows, span("own")]
            net.start(("gc", "D", h), gcs.at[1 - near, o, rows], to, dev["D"])
            net.start(("gc", "Y", h), gcs.at[near, o, rows], to, dev["Y"])
            net.start(("gc", "Z", h), gcs.at[1 - near, p, rows], to, dev["Z"])
            if h:
                gc_mine().start()

    for h in range(2):
        gc_out(h)

    rows = {"Y": slice(0, 384), "Z": slice(0, 384), "D": slice(128, 384), "own": slice(0, 512)}

    def products(b, js):
        s = slot[b]
        total = 0.0
        for j in js:
            rhs = gg[s, :, :, zc[j]].reshape(1024, 384)
            total = total + jnp.dot(ct[j, rows[b]], rhs, preferred_element_type=F32)
        return total

    slots = ("Y", "D", "own", "Z")

    def early(j, b):
        @task(f"e{j} {b}", after=(f"in{j} {b}", f"turn {j}", *((f"e{j - 1} {b}",) if j else ())))
        def _():
            at = (slot[b], rows[b])
            t = products(b, (j,))
            gw2[at] = gw2[at] + t if j else t

    for j in range(3):
        for b in slots:
            early(j, b)

    gw_copies = (
        pltpu.make_async_copy(gw2.at[slot["own"], slice(0, 384)], gw_ref.at[span("own")], local.at[4]),
        pltpu.make_async_copy(gw2.at[slot["own"], slice(384, 512)], gw_ref.at[third("D")], local.at[6]),
    )

    def late(b):
        @task(f"late {b}", after=(f"e2 {b}", "turn 3", f"in3 {b}"))
        def _():
            at = (slot[b], rows[b])
            gw2[at] = (gw2[at] + products(b, (3,))) * factor
            if b == "own":
                for copy in gw_copies:
                    copy.start()
            else:
                to = rest("own") if b == "D" else span("own")
                net.start(("gw", b), gw2.at[at], gw_ref.at[to], dev[b])

    for b in slots:
        late(b)

    @task("sent", after=("gc 1", *(f"late {b}" for b in slots)))
    def _():
        net.drain(later=("gc", "gw"))

    @task(
        "end",
        waits=[(("gw", b), gw_ref.at[rest(b) if b == "D" else span(b)]) for b in ("Y", "Z", "D")]
        + [(("gc", b, h), gc_ref.at[HALF[h], span(b)]) for b in ("Y", "Z", "D") for h in range(2)],
        after=("sent",),
    )
    def _():
        for copy in gw_copies:
            copy.wait()
        gc_mine().wait()

    run_tasks(tasks, net)
    net.drain()
    assert len(net.index) <= N_SEMS


def hand_over(gc_ref, gw_ref, gc_out, gw_out, gc_buf, gw_buf, read, written):
    rows = gw_ref.shape[0] // PIECES
    routes = [(gw_ref.at[pl.ds(i * rows, rows)], gw_buf.at[pl.ds(i * rows, rows)], gw_out.at[pl.ds(i * rows, rows)]) for i in range(PIECES)]
    routes.append((gc_ref, gc_buf, gc_out))
    reads = [pltpu.make_async_copy(a, b, read.at[i]) for i, (a, b, _) in enumerate(routes)]
    writes = [pltpu.make_async_copy(b, c, written.at[i]) for i, (_, b, c) in enumerate(routes)]
    for copy in reads:
        copy.start()
    for r, w in zip(reads, writes):
        r.wait()
        w.start()
    for copy in writes:
        copy.wait()


SCRATCH = (
    ((4, 2, 4, 128, 512), BF16),
    ((4, 512, 1024), BF16),
    ((4, 4, 2, 4, 128, 384), BF16),
    ((4, 384, 384), BF16),
    ((4, 2, 4, 128, 384), F32),
    ((4, 2, 128, 384), F32),
    ((4, 2, 2, 128, 384), F32),
    ((2, 128, 384), F32),
    ((4, 2, 128, 384), F32),
    ((4, 512, 384), F32),
    ((2, 2, 128, 384), BF16),
)


def on_device(context, out_weight, grad_out):
    factor = float(4096) ** (-0.5)
    anywhere = pl.BlockSpec(memory_space=pl.ANY)
    results = pl.pallas_call(
        functools.partial(kernel, factor),
        out_shape=(
            jax.ShapeDtypeStruct((128, 1536), BF16),
            jax.ShapeDtypeStruct((1536, 384), F32),
        ),
        in_specs=[anywhere] * 3,
        out_specs=(anywhere, anywhere),
        scratch_shapes=[
            *(pltpu.VMEM(shape, dtype) for shape, dtype in SCRATCH),
            pltpu.SemaphoreType.DMA((N_SEMS,)),
            pltpu.SemaphoreType.DMA((N_SEMS,)),
            pltpu.SemaphoreType.DMA((7,)),
        ],
        compiler_params=pltpu.CompilerParams(
            collective_id=0, has_side_effects=True, vmem_limit_bytes=60 * 2**20
        ),
        cost_estimate=pl.CostEstimate(flops=9663676416, bytes_accessed=5111808, transcendentals=0),
        name="both_gradients",
    )(context, out_weight, grad_out.reshape(2, 4, 128, 384))
    return pl.pallas_call(
        hand_over,
        out_shape=tuple(jax.ShapeDtypeStruct(r.shape, r.dtype) for r in results),
        in_specs=[anywhere] * 2,
        out_specs=(anywhere, anywhere),
        scratch_shapes=[
            pltpu.VMEM((128, 1536), BF16),
            pltpu.VMEM((1536, 384), F32),
            pltpu.SemaphoreType.DMA((1 + PIECES,)),
            pltpu.SemaphoreType.DMA((1 + PIECES,)),
        ],
        cost_estimate=pl.CostEstimate(flops=0, bytes_accessed=5505024, transcendentals=0),
        name="hand_over",
    )(*results)


def solution(mesh):
    fine = Mesh(mesh.devices.reshape(4, 2, 4, 2, 2), AXES)
    dp, tensor = ("x", "ylo", "z"), ("yhi", "core")
    return jax.shard_map(
        on_device,
        mesh=fine,
        in_specs=(P(dp, tensor), P(tensor, dp), P(tensor, dp)),
        out_specs=(P(dp, tensor), P(tensor, dp)),
        check_vma=False,
    )
```

```python
import functools

import jax
import jax.numpy as jnp
from jax import lax
from jax.experimental import pallas as pl
from jax.experimental.pallas import tpu as pltpu
from jax.sharding import Mesh
from jax.sharding import PartitionSpec as P

AXES = ("x", "ylo", "z", "yhi", "core")
BF16 = jnp.bfloat16
F32 = jnp.float32
N_SEMS = 240
PIECES = 4
HALF = (slice(0, 64), slice(64, 128))
X_FIRST = ("own", "Y")
MAIN, EXTRA = slice(0, 384), slice(384, 512)
ORDER = (
    4, 0, 1, 45, 44, 94, 2, 46, 117, 5, 114, 68, 3, 8, 19, 69, 70, 7, 6, 48, 53, 11, 71, 54, 72, 77, 23, 17, 41,
    42, 18, 51, 55, 43, 56, 50, 74, 22, 78, 28, 79, 47, 116, 20, 57, 24, 31, 30, 93, 49, 73, 115, 59, 25, 62,
    75, 34, 21, 60, 84, 13, 124, 32, 58, 92, 26, 36, 52, 12, 35, 14, 61, 76, 27, 91, 63, 66, 82, 16, 9, 80, 85,
    65, 81, 15, 33, 86, 83, 10, 87, 40, 39, 157, 118, 158, 29, 64, 123, 159, 88, 89, 162, 126, 120, 119, 100,
    101, 121, 90, 129, 95, 141, 142, 161, 127, 125, 38, 128, 132, 122, 102, 156, 107, 130, 104, 143, 131, 133,
    98, 160, 96, 134, 37, 109, 97, 165, 135, 169, 136, 103, 67, 164, 105, 99, 144, 150, 151, 163, 108, 106, 110,
    112, 167, 168, 137, 111, 113, 171, 166, 139, 170, 138, 146, 145, 140, 147, 148, 152, 153, 154, 149, 155,
    172, 173,
)
LATE_ROUTE = (3,)


class Links:
    def __init__(self, send, recv, anyone):
        self.send, self.recv, self.anyone = send, recv, anyone
        self.index, self.started = {}, {}

    def slot(self, name):
        return self.index.setdefault(name, len(self.index))

    def start(self, name, src, dst, device):
        i = self.slot(name)
        copy = pltpu.make_async_remote_copy(
            src_ref=src, dst_ref=dst, send_sem=self.send.at[i], recv_sem=self.recv.at[i],
            device_id=device, device_id_type=pl.DeviceIdType.MESH,
        )
        copy.start()
        self.started[name] = src

    def wait(self, name, dst):
        i = self.slot(name)
        pltpu.make_async_remote_copy(
            src_ref=dst, dst_ref=dst, send_sem=self.send.at[i], recv_sem=self.recv.at[i],
            device_id=self.anyone, device_id_type=pl.DeviceIdType.MESH,
        ).wait_recv()

    def drain(self, later=()):
        for name in [n for n in self.started if n[0] not in later]:
            i, sent = self.index[name], self.started.pop(name)
            pltpu.make_async_remote_copy(
                src_ref=sent, dst_ref=sent, send_sem=self.send.at[i], recv_sem=self.recv.at[i],
                device_id=self.anyone, device_id_type=pl.DeviceIdType.MESH,
            ).wait_send()


def run_tasks(tasks, net):
    assert len(ORDER) == len(tasks)
    listed = list(tasks.values())
    for i in ORDER:
        waits, body, _ = listed[i]
        for what, where in waits:
            net.wait(what, where)
        body()


def kernel(factor, c_ref, w_ref, g_ref, gc_ref, gw_ref, cg, ct, gg, wb, part, r1, r2, qz, fz, gw2, gcs, send, recv, local):
    x, p, z, q, core = (lax.axis_index(a) for a in AXES)
    o = 1 - p
    z_near = z + 1 - 2 * lax.rem(z, 2)
    z_far = 3 - z
    zd = lax.rem(lax.div(z + 1, 2), 2)
    zg = lax.div(z, 2)

    x_up, x_down = (lax.rem(x + 1, 4), p, z, q, core), (lax.rem(x + 3, 4), p, z, q, core)
    dev = {
        "Y": (x, o, z, q, core),
        "Z": (x, p, z_near, q, core),
        "D": (x, o, z_near, q, core),
        "C": (x, o, z, 1 - q, core),
        "T": (x, p, z, q, 1 - core),
        "F": (x, p, z_far, q, core),
    }
    barrier = pltpu.get_barrier_semaphore()
    everyone = (x_up, x_down, *dev.values())
    for other in everyone:
        pl.semaphore_signal(barrier, inc=1, device_id=other, device_id_type=pl.DeviceIdType.MESH)

    net = Links(send, recv, dev["T"])
    xs = [lax.rem(x + d, 4) for d in range(4)]
    slot = {"own": 2 * p + zd, "Y": 2 * o + zd, "Z": 2 * p + 1 - zd, "D": 2 * o + 1 - zd}
    home = {"own": (p, z), "Y": (o, z), "Z": (p, z_near), "D": (o, z_near)}
    far = {b: (pp, 3 - zz) for b, (pp, zz) in home.items()}

    opposite = {"own": "D", "Y": "Z", "Z": "Y", "D": "own"}

    def third(b):
        return pl.ds(pl.multiple_of(384 * slot[b], 128), 128)

    def rest(b):
        return pl.ds(pl.multiple_of(384 * slot[b] + 128, 128), 256)

    def span(b):
        return pl.ds(pl.multiple_of(384 * slot[b], 128), 384)

    k_own, k_cross = 2 * q + core, 2 * (1 - q) + core
    k_twin, k_far = 2 * q + 1 - core, 2 * (1 - q) + 1 - core
    zc = [2 * (1 - zg), 2 * (1 - zg) + 1, 2 * zg, 2 * zg + 1]

    tasks = {}

    def task(name, waits=(), after=()):
        def add(body):
            tasks[name] = (tuple(waits), body, tuple(after))
            return body

        return add

    def c_to(b):
        @task(f"ca {b}")
        def _():
            net.start(("ca", b), c_ref.at[:, span(b)], cg.at[x, p, z, :, MAIN], dev[b])
            net.start(("cb", b), c_ref.at[:, third(opposite[b])], cg.at[x, p, z, :, EXTRA], dev[b])

    for b in ("D", "Y", "Z"):
        c_to(b)

    @task("c0", after=("locals done",))
    def _():
        mine = cg.at[x, p, z]
        net.start(("cz", 0, "own"), mine, mine, dev["F"])
        for name, device in (("x+", x_up), ("x-", x_down)):
            net.start(("cx", name, "own"), mine, mine, device)

    copies = [
        pltpu.make_async_copy(c_ref.at[:, span("own")], cg.at[x, p, z, :, MAIN], local.at[0]),
        pltpu.make_async_copy(c_ref.at[:, third("D")], cg.at[x, p, z, :, EXTRA], local.at[5]),
        pltpu.make_async_copy(g_ref, gg.at[slot["own"], k_own], local.at[1]),
        pltpu.make_async_copy(w_ref.at[span("own")], wb.at[slot["own"]], local.at[2]),
    ]

    for copy in copies:
        copy.start()
    pl.semaphore_wait(barrier, len(everyone))

    @task("locals")
    def _():
        pass

    @task("locals done", after=("locals",))
    def _():
        for copy in copies:
            copy.wait()

    place = {**home, **{f"f{b}": at for b, at in far.items()}}

    def c_round(b):
        block = cg.at[(x, *place[b])]
        for name, device in (("x+", x_up), ("x-", x_down)):
            net.start(("cx", name, b), block, block, device)

    def c_gather(b):
        block = cg.at[(x, *place[b])]

        waits = [(("ca", b), cg.at[(x, *place[b], slice(None), MAIN)]), (("cb", b), cg.at[(x, *place[b], slice(None), EXTRA)])]

        @task(f"c {b}", waits=waits, after=("c0", f"ca {b}"))
        def _():
            net.start(("cz", 0, b), block, block, dev["F"])
            c_round(b)

    def c_across(b):
        @task(f"c f{b}", waits=[(("cz", 0, b), cg.at[(x, *far[b])])], after=("c0",) if b == "own" else (f"c {b}",))
        def _():
            if b not in X_FIRST:
                c_round(f"f{b}")

        def from_far(dx, after):
            @task(f"c f{b}{dx}", waits=[(("cz", dx, b), cg.at[(xs[dx], *far[b])])], after=(after,))
            def _():
                pass

        if b in X_FIRST:
            for dx, after in ((1, f"c x- {b}"), (3, f"c x+ {b}"), (2, f"c last {b}")):
                from_far(dx, after)

    def c_pass(name, b):
        dx, device = (3, x_up) if name == "x+" else (1, x_down)
        block, last = cg.at[(xs[dx], *place[b])], cg.at[(xs[2], *place[b])]
        on = (b[-1] in "nD") == (name == "x+")

        @task(f"c {name} {b}", waits=[(("cx", name, b), block)], after=("c0",) if b == "own" else (f"c {b}",))
        def _():
            if on:
                net.start(("cf", b), block, block, device)
            if b in X_FIRST:
                net.start(("cz", dx, b), block, block, dev["F"])

        if on:

            @task(f"c last {b}", waits=[(("cf", b), last)], after=(f"c {name} {b}",))
            def _():
                if b in X_FIRST:
                    net.start(("cz", 2, b), last, last, dev["F"])

    for b in ("Y", "Z", "D"):
        c_gather(b)
    for b in home:
        c_across(b)
    rounds = [b for b in place if b[1:] not in X_FIRST]
    for b in rounds:
        c_pass("x+", b)
        c_pass("x-", b)

    def turned(j):
        ct[j] = cg[:, :, zc[j]].reshape(1024, 512).T

    for pre in ("", "f"):
        names = [f"c {n} {pre}{b}" for n in ("x+", "x-", "last") for b in home if pre + b in rounds]
        names += [f"c {pre}{b}" for b in home if pre + b != "own"]
        names += [f"c f{b}{dx}" for b in X_FIRST for dx in (1, 2, 3) if pre]
        for j in (2, 3) if pre == "" else (0, 1):

            @task(f"turn {j}", after=(*names, "locals done"))
            def _(j=j):
                turned(j)

    def w_to(b):
        @task(f"w {b}")
        def _():
            net.start(("w", b), w_ref.at[span(b)], wb.at[slot["own"]], dev[b])

    for b in ("D", "Y", "Z"):
        w_to(b)

    def round_x(j, d):
        zz = zc[j]
        if d == 2:
            net.start(("r1 L", j), part.at[xs[2], 0, zz], r1.at[j, 0], x_down)
            net.start(("r1 R", j), part.at[xs[2], 1, zz], r1.at[j, 1], x_up)
        elif d == 3:
            net.start(("r2 +", j, 1), part.at[xs[3], 1, zz], r2.at[j, 0, 1], x_down)
        elif d == 1:
            net.start(("r2 -", j, 0), part.at[xs[1], 0, zz], r2.at[j, 1, 0], x_up)

    def g_tasks(j):
        zz = zc[j]
        both = slice(None)

        def at(b, k, pp):
            return gg.at[slot[b], k, pp, zz]

        def fwd(to, b, k, pp):
            net.start(("g", j, to, b, k, pp if isinstance(pp, int) else 2), at(b, K[k], pp), at(b, K[k], pp), dev[to])

        K = {"h": k_own, "c": k_cross}
        H = {"h": k_twin, "c": k_far}

        heard = {b: [] for b in home}
        here = {b: [] for b in home}

        def own_to(to):
            @task(f"g{j} own{to}")
            def _():
                net.start(("g", j, to, "own", "h", 2), g_ref.at[:, zz], gg.at[slot["own"], k_own, :, zz], dev[to])

        for to in ("C", "Y", "Z", "T"):
            own_to(to)

        heard["own"].append((("g", j, "T", "own", "h", 2), at("own", k_twin, both)))

        def got(name, to, sent, b, k, pp, sends):
            heard[b].append((("g", j, "T", b, k, pp if isinstance(pp, int) else 2), at(b, H[k], pp)))
            here[b].append(f"g{j} {name}")
            key = ("g", j, to, *sent, pp if isinstance(pp, int) else 2)

            @task(f"g{j} {name}", waits=[(key, at(b, K[k], pp))], after=(f"g{j} own{to}",))
            def _():
                for dest, part_p in sends:
                    fwd(dest, b, k, part_p)
                fwd("T", b, k, pp)

        late_route = j in LATE_ROUTE
        got("Y", "Y", ("own", "h"), "Y", "h", both, (("C", 1), ("Z", 1)))
        got("YZ1", "Z", ("Y", "h"), "D", "h", 1, (("C", 1),))
        got("YC1", "C", ("Y", "h"), "own", "c", 1, ())
        got("ZC1", "C", ("Z", "h"), "D", "c", 1, ())
        got("YZC1", "C", ("D", "h"), "Z", "c", 1, ())
        if late_route:
            got("Z", "Z", ("own", "h"), "Z", "h", both, (("C", 1), ("Y", 0), ("C", 0)))
            got("C", "C", ("own", "h"), "Y", "c", both, (("Y", 0),))
            got("YZ0", "Y", ("Z", "h"), "D", "h", 0, ())
            got("YC0", "Y", ("Y", "c"), "own", "c", 0, (("Z", 0),))
            got("ZC0", "C", ("Z", "h"), "D", "c", 0, ())
            got("YZC0", "Z", ("own", "c"), "Z", "c", 0, ())
        else:
            got("Z", "Z", ("own", "h"), "Z", "h", both, (("C", 1), ("Y", 0)))
            got("C", "C", ("own", "h"), "Y", "c", both, (("Y", 0), ("Z", 0)))
            got("YZ0", "Y", ("Z", "h"), "D", "h", 0, (("C", 0),))
            got("YC0", "Y", ("Y", "c"), "own", "c", 0, ())
            got("ZC0", "Z", ("Y", "c"), "D", "c", 0, ())
            got("YZC0", "C", ("D", "h"), "Z", "c", 0, ())

        def slot_in(b):
            @task(f"in{j} {b}", waits=heard[b], after=(*here[b], f"g{j} ownT", "locals done"))
            def _():
                pass

        for b in home:
            slot_in(b)
        if j == 0:

            @task("w in", waits=[(("w", b), wb.at[slot[b]]) for b in ("D", "Y", "Z")], after=("w D", "w Y", "w Z", "locals done"))
            def _():
                pass

        def sums(d):
            @task(f"s{j} {d}", after=("w in", *(f"in{j} {b}" for b in home)))
            def _():
                weight = jnp.concatenate([wb[s] for s in range(4)], axis=1)
                r = jnp.concatenate([gg[s, xs[d], :, zz].reshape(256, 384) for s in range(4)], axis=1)
                t = lax.dot_general(r, weight, (((1,), (1,)), ((), ())), preferred_element_type=F32)
                part[xs[d], :, zz] = t.reshape(2, 128, 384)
                if j == 0:
                    net.start(("fz", d), part.at[xs[d], :, zz], fz.at[d], dev["F"])
                elif j != 2:
                    round_x(j, d)

        for d in (2, 1, 3, 0):
            sums(d)

    for j in range(4):
        g_tasks(j)

    def across(d):
        zz = zc[2]

        @task(f"f {d}", waits=[(("fz", d), fz.at[d])], after=("s0 0", f"s2 {d}"))
        def _():
            part[xs[d], :, zz] = part[xs[d], :, zz] + fz[d]
            round_x(2, d)

    for d in (2, 1, 3, 0):
        across(d)

    near = lax.rem(z, 2)

    def gc_mine():
        return pltpu.make_async_copy(gcs.at[near, p], gc_ref.at[:, span("own")], local.at[3])

    def reduce_tasks(j):
        zz = zc[j]
        ready = {3: "f 3", 1: "f 1", 0: "f 0"} if j == 2 else {d: f"s{j} {d}" for d in (3, 1, 0)}
        pieces = HALF if j == 2 else (slice(0, 128),)

        @task(f"r L {j}", waits=[(("r1 L", j), r1.at[j, 0])], after=(ready[3],))
        def _():
            part[xs[3], 0, zz] = part[xs[3], 0, zz] + r1[j, 0]
            for h, rows in enumerate(pieces):
                net.start(("r2 +", j, 0, h), part.at[xs[3], 0, zz, rows], r2.at[j, 0, 0, rows], x_down)

        @task(f"r R {j}", waits=[(("r1 R", j), r1.at[j, 1])], after=(ready[1],))
        def _():
            part[xs[1], 1, zz] = part[xs[1], 1, zz] + r1[j, 1]
            for h, rows in enumerate(pieces):
                net.start(("r2 -", j, 1, h), part.at[xs[1], 1, zz, rows], r2.at[j, 1, 1, rows], x_up)

        waits = [(("r2 +", j, 1), r2.at[j, 0, 1]), (("r2 -", j, 0), r2.at[j, 1, 0])]
        if j == 3:
            waits.append((("qz", 0), qz))

        @task(f"r {j} d", waits=waits, after=(ready[0], *(("r 1 0",) if j == 3 else ())))
        def _():
            pass

        def total(h, rows):
            waits = [(("r2 +", j, 0, h), r2.at[j, 0, 0, rows]), (("r2 -", j, 1, h), r2.at[j, 1, 1, rows])]

            @task(f"r {j} {h}", waits=waits, after=(f"r L {j}", f"r R {j}", f"r {j} d"))
            def _():
                t = part[x, :, zz, rows] + r2[j, 0, :, rows] + r2[j, 1, :, rows]
                if j == 1:
                    part[x, :, zz, rows] = t
                    net.start(("qz", 0), part.at[x, :, zz], qz, dev["F"])
                else:
                    gcs[j - 2, :, rows] = (t if j == 2 else t + qz[:, rows]).astype(BF16)

        for h, rows in enumerate(pieces):
            total(h, rows)

    for j in (1, 2, 3):
        reduce_tasks(j)

    def gc_out(h):
        rows = HALF[h]

        @task(f"gc {h}", after=(f"r 2 {h}", "r 3 0", *(("gc 0",) if h else ())))
        def _():
            to = gc_ref.at[rows, span("own")]
            net.start(("gc", "D", h), gcs.at[1 - near, o, rows], to, dev["D"])
            net.start(("gc", "Y", h), gcs.at[near, o, rows], to, dev["Y"])
            net.start(("gc", "Z", h), gcs.at[1 - near, p, rows], to, dev["Z"])
            if h:
                gc_mine().start()

    for h in range(2):
        gc_out(h)

    rows = {"Y": slice(0, 384), "Z": slice(0, 384), "D": slice(128, 384), "own": slice(0, 512)}

    def products(b, js):
        s = slot[b]
        total = 0.0
        for j in js:
            rhs = gg[s, :, :, zc[j]].reshape(1024, 384)
            total = total + jnp.dot(ct[j, rows[b]], rhs, preferred_element_type=F32)
        return total

    slots = ("Y", "D", "own", "Z")

    def early(j, b):
        @task(f"e{j} {b}", after=(f"in{j} {b}", f"turn {j}", *((f"e{j - 1} {b}",) if j else ())))
        def _():
            at = (slot[b], rows[b])
            t = products(b, (j,))
            gw2[at] = gw2[at] + t if j else t

    for j in range(3):
        for b in slots:
            early(j, b)

    gw_copies = (
        pltpu.make_async_copy(gw2.at[slot["own"], slice(0, 384)], gw_ref.at[span("own")], local.at[4]),
        pltpu.make_async_copy(gw2.at[slot["own"], slice(384, 512)], gw_ref.at[third("D")], local.at[6]),
    )

    def late(b):
        @task(f"late {b}", after=(f"e2 {b}", "turn 3", f"in3 {b}"))
        def _():
            at = (slot[b], rows[b])
            gw2[at] = (gw2[at] + products(b, (3,))) * factor
            if b == "own":
                for copy in gw_copies:
                    copy.start()
            else:
                to = rest("own") if b == "D" else span("own")
                net.start(("gw", b), gw2.at[at], gw_ref.at[to], dev[b])

    for b in slots:
        late(b)

    @task("sent", after=("gc 1", *(f"late {b}" for b in slots)))
    def _():
        net.drain(later=("gc", "gw"))

    @task(
        "end",
        waits=[(("gw", b), gw_ref.at[rest(b) if b == "D" else span(b)]) for b in ("Y", "Z", "D")]
        + [(("gc", b, h), gc_ref.at[HALF[h], span(b)]) for b in ("Y", "Z", "D") for h in range(2)],
        after=("sent",),
    )
    def _():
        for copy in gw_copies:
            copy.wait()
        gc_mine().wait()

    run_tasks(tasks, net)
    net.drain()
    assert len(net.index) <= N_SEMS


def hand_over(gc_ref, gw_ref, gc_out, gw_out, gc_buf, gw_buf, read, written):
    rows = gw_ref.shape[0] // PIECES
    routes = [(gw_ref.at[pl.ds(i * rows, rows)], gw_buf.at[pl.ds(i * rows, rows)], gw_out.at[pl.ds(i * rows, rows)]) for i in range(PIECES)]
    routes.append((gc_ref, gc_buf, gc_out))
    reads = [pltpu.make_async_copy(a, b, read.at[i]) for i, (a, b, _) in enumerate(routes)]
    writes = [pltpu.make_async_copy(b, c, written.at[i]) for i, (_, b, c) in enumerate(routes)]
    for copy in reads:
        copy.start()
    for r, w in zip(reads, writes):
        r.wait()
        w.start()
    for copy in writes:
        copy.wait()


SCRATCH = (
    ((4, 2, 4, 128, 512), BF16),
    ((4, 512, 1024), BF16),
    ((4, 4, 2, 4, 128, 384), BF16),
    ((4, 384, 384), BF16),
    ((4, 2, 4, 128, 384), F32),
    ((4, 2, 128, 384), F32),
    ((4, 2, 2, 128, 384), F32),
    ((2, 128, 384), F32),
    ((4, 2, 128, 384), F32),
    ((4, 512, 384), F32),
    ((2, 2, 128, 384), BF16),
)


def on_device(context, out_weight, grad_out):
    factor = float(4096) ** (-0.5)
    anywhere = pl.BlockSpec(memory_space=pl.ANY)
    results = pl.pallas_call(
        functools.partial(kernel, factor),
        out_shape=(
            jax.ShapeDtypeStruct((128, 1536), BF16),
            jax.ShapeDtypeStruct((1536, 384), F32),
        ),
        in_specs=[anywhere] * 3,
        out_specs=(anywhere, anywhere),
        scratch_shapes=[
            *(pltpu.VMEM(shape, dtype) for shape, dtype in SCRATCH),
            pltpu.SemaphoreType.DMA((N_SEMS,)),
            pltpu.SemaphoreType.DMA((N_SEMS,)),
            pltpu.SemaphoreType.DMA((7,)),
        ],
        compiler_params=pltpu.CompilerParams(
            collective_id=0, has_side_effects=True, vmem_limit_bytes=60 * 2**20
        ),
        cost_estimate=pl.CostEstimate(flops=9663676416, bytes_accessed=5111808, transcendentals=0),
        name="both_gradients",
    )(context, out_weight, grad_out.reshape(2, 4, 128, 384))
    return pl.pallas_call(
        hand_over,
        out_shape=tuple(jax.ShapeDtypeStruct(r.shape, r.dtype) for r in results),
        in_specs=[anywhere] * 2,
        out_specs=(anywhere, anywhere),
        scratch_shapes=[
            pltpu.VMEM((128, 1536), BF16),
            pltpu.VMEM((1536, 384), F32),
            pltpu.SemaphoreType.DMA((1 + PIECES,)),
            pltpu.SemaphoreType.DMA((1 + PIECES,)),
        ],
        cost_estimate=pl.CostEstimate(flops=0, bytes_accessed=5505024, transcendentals=0),
        name="hand_over",
    )(*results)


def solution(mesh):
    fine = Mesh(mesh.devices.reshape(4, 2, 4, 2, 2), AXES)
    dp, tensor = ("x", "ylo", "z"), ("yhi", "core")
    return jax.shard_map(
        on_device,
        mesh=fine,
        in_specs=(P(dp, tensor), P(tensor, dp), P(tensor, dp)),
        out_specs=(P(dp, tensor), P(tensor, dp)),
        check_vma=False,
    )
```

```python
import functools

import jax
import jax.numpy as jnp
from jax import lax
from jax.experimental import pallas as pl
from jax.experimental.pallas import tpu as pltpu
from jax.sharding import Mesh
from jax.sharding import PartitionSpec as P

AXES = ("x", "ylo", "z", "yhi", "core")
BF16 = jnp.bfloat16
F32 = jnp.float32
N_SEMS = 240
PIECES = 4
HALF = (slice(0, 64), slice(64, 128))
X_FIRST = ("own", "Y")
MAIN, EXTRA = slice(0, 384), slice(384, 512)
ORDER = (
    4, 0, 1, 45, 44, 94, 2, 46, 117, 5, 114, 68, 3, 8, 19, 69, 70, 7, 6, 48, 53, 11, 71, 54, 72, 77, 23, 17, 41,
    42, 18, 51, 55, 43, 56, 50, 74, 22, 78, 28, 79, 47, 116, 20, 57, 24, 31, 30, 93, 49, 73, 115, 59, 25, 62,
    75, 34, 21, 60, 84, 13, 124, 32, 58, 92, 26, 36, 52, 12, 35, 14, 61, 76, 27, 91, 63, 66, 82, 16, 9, 80, 85,
    65, 81, 15, 33, 86, 83, 10, 87, 40, 39, 157, 118, 158, 29, 64, 123, 159, 88, 89, 162, 126, 120, 119, 100,
    101, 121, 90, 129, 95, 141, 142, 161, 127, 125, 38, 128, 132, 122, 102, 156, 107, 130, 104, 143, 131, 133,
    98, 160, 96, 134, 37, 109, 97, 165, 135, 169, 136, 103, 67, 164, 105, 99, 144, 150, 151, 163, 108, 106, 110,
    112, 167, 168, 137, 111, 113, 171, 166, 139, 170, 138, 146, 145, 140, 147, 148, 152, 153, 154, 149, 155,
    172, 173,
)
LATE_ROUTE = (3,)


class Links:
    def __init__(self, send, recv, anyone):
        self.send, self.recv, self.anyone = send, recv, anyone
        self.index, self.started = {}, {}

    def slot(self, name):
        return self.index.setdefault(name, len(self.index))

    def start(self, name, src, dst, device):
        i = self.slot(name)
        copy = pltpu.make_async_remote_copy(
            src_ref=src, dst_ref=dst, send_sem=self.send.at[i], recv_sem=self.recv.at[i],
            device_id=device, device_id_type=pl.DeviceIdType.MESH,
        )
        copy.start()
        self.started[name] = src

    def wait(self, name, dst):
        i = self.slot(name)
        pltpu.make_async_remote_copy(
            src_ref=dst, dst_ref=dst, send_sem=self.send.at[i], recv_sem=self.recv.at[i],
            device_id=self.anyone, device_id_type=pl.DeviceIdType.MESH,
        ).wait_recv()

    def drain(self, later=()):
        for name in [n for n in self.started if n[0] not in later]:
            i, sent = self.index[name], self.started.pop(name)
            pltpu.make_async_remote_copy(
                src_ref=sent, dst_ref=sent, send_sem=self.send.at[i], recv_sem=self.recv.at[i],
                device_id=self.anyone, device_id_type=pl.DeviceIdType.MESH,
            ).wait_send()


def run_tasks(tasks, net):
    assert len(ORDER) == len(tasks)
    listed = list(tasks.values())
    for i in ORDER:
        waits, body, _ = listed[i]
        for what, where in waits:
            net.wait(what, where)
        body()


def kernel(factor, c_ref, w_ref, g_ref, gc_ref, gw_ref, cg, ct, gg, wb, part, r1, r2, qz, fz, gw2, gcs, send, recv, local):
    x, p, z, q, core = (lax.axis_index(a) for a in AXES)
    o = 1 - p
    z_near = z + 1 - 2 * lax.rem(z, 2)
    z_far = 3 - z
    zd = lax.rem(lax.div(z + 1, 2), 2)
    zg = lax.div(z, 2)

    x_up, x_down = (lax.rem(x + 1, 4), p, z, q, core), (lax.rem(x + 3, 4), p, z, q, core)
    dev = {
        "Y": (x, o, z, q, core),
        "Z": (x, p, z_near, q, core),
        "D": (x, o, z_near, q, core),
        "C": (x, o, z, 1 - q, core),
        "T": (x, p, z, q, 1 - core),
        "F": (x, p, z_far, q, core),
    }
    barrier = pltpu.get_barrier_semaphore()
    everyone = (x_up, x_down, *dev.values())
    for other in everyone:
        pl.semaphore_signal(barrier, inc=1, device_id=other, device_id_type=pl.DeviceIdType.MESH)

    net = Links(send, recv, dev["T"])
    xs = [lax.rem(x + d, 4) for d in range(4)]
    slot = {"own": 2 * p + zd, "Y": 2 * o + zd, "Z": 2 * p + 1 - zd, "D": 2 * o + 1 - zd}
    home = {"own": (p, z), "Y": (o, z), "Z": (p, z_near), "D": (o, z_near)}
    far = {b: (pp, 3 - zz) for b, (pp, zz) in home.items()}

    opposite = {"own": "D", "Y": "Z", "Z": "Y", "D": "own"}

    def third(b):
        return pl.ds(pl.multiple_of(384 * slot[b], 128), 128)

    def rest(b):
        return pl.ds(pl.multiple_of(384 * slot[b] + 128, 128), 256)

    def span(b):
        return pl.ds(pl.multiple_of(384 * slot[b], 128), 384)

    k_own, k_cross = 2 * q + core, 2 * (1 - q) + core
    k_twin, k_far = 2 * q + 1 - core, 2 * (1 - q) + 1 - core
    zc = [2 * (1 - zg), 2 * (1 - zg) + 1, 2 * zg, 2 * zg + 1]

    tasks = {}

    def task(name, waits=(), after=()):
        def add(body):
            tasks[name] = (tuple(waits), body, tuple(after))
            return body

        return add

    def c_to(b):
        @task(f"ca {b}")
        def _():
            net.start(("ca", b), c_ref.at[:, span(b)], cg.at[x, p, z, :, MAIN], dev[b])
            net.start(("cb", b), c_ref.at[:, third(opposite[b])], cg.at[x, p, z, :, EXTRA], dev[b])

    for b in ("D", "Y", "Z"):
        c_to(b)

    @task("c0", after=("locals done",))
    def _():
        mine = cg.at[x, p, z]
        net.start(("cz", 0, "own"), mine, mine, dev["F"])
        for name, device in (("x+", x_up), ("x-", x_down)):
            net.start(("cx", name, "own"), mine, mine, device)

    copies = [
        pltpu.make_async_copy(c_ref.at[:, span("own")], cg.at[x, p, z, :, MAIN], local.at[0]),
        pltpu.make_async_copy(c_ref.at[:, third("D")], cg.at[x, p, z, :, EXTRA], local.at[5]),
        pltpu.make_async_copy(g_ref, gg.at[slot["own"], k_own], local.at[1]),
        pltpu.make_async_copy(w_ref.at[span("own")], wb.at[slot["own"]], local.at[2]),
    ]

    for copy in copies:
        copy.start()
    pl.semaphore_wait(barrier, len(everyone))

    @task("locals")
    def _():
        pass

    @task("locals done", after=("locals",))
    def _():
        for copy in copies:
            copy.wait()

    place = {**home, **{f"f{b}": at for b, at in far.items()}}

    def c_round(b):
        block = cg.at[(x, *place[b])]
        for name, device in (("x+", x_up), ("x-", x_down)):
            net.start(("cx", name, b), block, block, device)

    def c_gather(b):
        block = cg.at[(x, *place[b])]

        waits = [(("ca", b), cg.at[(x, *place[b], slice(None), MAIN)]), (("cb", b), cg.at[(x, *place[b], slice(None), EXTRA)])]

        @task(f"c {b}", waits=waits, after=("c0", f"ca {b}"))
        def _():
            net.start(("cz", 0, b), block, block, dev["F"])
            c_round(b)

    def c_across(b):
        @task(f"c f{b}", waits=[(("cz", 0, b), cg.at[(x, *far[b])])], after=("c0",) if b == "own" else (f"c {b}",))
        def _():
            if b not in X_FIRST:
                c_round(f"f{b}")

        def from_far(dx, after):
            @task(f"c f{b}{dx}", waits=[(("cz", dx, b), cg.at[(xs[dx], *far[b])])], after=(after,))
            def _():
                pass

        if b in X_FIRST:
            for dx, after in ((1, f"c x- {b}"), (3, f"c x+ {b}"), (2, f"c last {b}")):
                from_far(dx, after)

    def c_pass(name, b):
        dx, device = (3, x_up) if name == "x+" else (1, x_down)
        block, last = cg.at[(xs[dx], *place[b])], cg.at[(xs[2], *place[b])]
        on = (b[-1] in "nD") == (name == "x+")

        @task(f"c {name} {b}", waits=[(("cx", name, b), block)], after=("c0",) if b == "own" else (f"c {b}",))
        def _():
            if on:
                net.start(("cf", b), block, block, device)
            if b in X_FIRST:
                net.start(("cz", dx, b), block, block, dev["F"])

        if on:

            @task(f"c last {b}", waits=[(("cf", b), last)], after=(f"c {name} {b}",))
            def _():
                if b in X_FIRST:
                    net.start(("cz", 2, b), last, last, dev["F"])

    for b in ("Y", "Z", "D"):
        c_gather(b)
    for b in home:
        c_across(b)
    rounds = [b for b in place if b[1:] not in X_FIRST]
    for b in rounds:
        c_pass("x+", b)
        c_pass("x-", b)

    def turned(j):
        ct[j] = cg[:, :, zc[j]].reshape(1024, 512).T

    for pre in ("", "f"):
        names = [f"c {n} {pre}{b}" for n in ("x+", "x-", "last") for b in home if pre + b in rounds]
        names += [f"c {pre}{b}" for b in home if pre + b != "own"]
        names += [f"c f{b}{dx}" for b in X_FIRST for dx in (1, 2, 3) if pre]
        for j in (2, 3) if pre == "" else (0, 1):

            @task(f"turn {j}", after=(*names, "locals done"))
            def _(j=j):
                turned(j)

    def w_to(b):
        @task(f"w {b}")
        def _():
            net.start(("w", b), w_ref.at[span(b)], wb.at[slot["own"]], dev[b])

    for b in ("D", "Y", "Z"):
        w_to(b)

    def round_x(j, d):
        zz = zc[j]
        if d == 2:
            net.start(("r1 L", j), part.at[xs[2], 0, zz], r1.at[j, 0], x_down)
            net.start(("r1 R", j), part.at[xs[2], 1, zz], r1.at[j, 1], x_up)
        elif d == 3:
            net.start(("r2 +", j, 1), part.at[xs[3], 1, zz], r2.at[j, 0, 1], x_down)
        elif d == 1:
            net.start(("r2 -", j, 0), part.at[xs[1], 0, zz], r2.at[j, 1, 0], x_up)

    def g_tasks(j):
        zz = zc[j]
        both = slice(None)

        def at(b, k, pp):
            return gg.at[slot[b], k, pp, zz]

        def fwd(to, b, k, pp):
            net.start(("g", j, to, b, k, pp if isinstance(pp, int) else 2), at(b, K[k], pp), at(b, K[k], pp), dev[to])

        K = {"h": k_own, "c": k_cross}
        H = {"h": k_twin, "c": k_far}

        heard = {b: [] for b in home}
        here = {b: [] for b in home}

        def own_to(to):
            @task(f"g{j} own{to}")
            def _():
                net.start(("g", j, to, "own", "h", 2), g_ref.at[:, zz], gg.at[slot["own"], k_own, :, zz], dev[to])

        for to in ("C", "Y", "Z", "T"):
            own_to(to)

        heard["own"].append((("g", j, "T", "own", "h", 2), at("own", k_twin, both)))

        def got(name, to, sent, b, k, pp, sends):
            heard[b].append((("g", j, "T", b, k, pp if isinstance(pp, int) else 2), at(b, H[k], pp)))
            here[b].append(f"g{j} {name}")
            key = ("g", j, to, *sent, pp if isinstance(pp, int) else 2)

            @task(f"g{j} {name}", waits=[(key, at(b, K[k], pp))], after=(f"g{j} own{to}",))
            def _():
                for dest, part_p in sends:
                    fwd(dest, b, k, part_p)
                fwd("T", b, k, pp)

        late_route = j in LATE_ROUTE
        got("Y", "Y", ("own", "h"), "Y", "h", both, (("C", 1), ("Z", 1)))
        got("YZ1", "Z", ("Y", "h"), "D", "h", 1, (("C", 1),))
        got("YC1", "C", ("Y", "h"), "own", "c", 1, ())
        got("ZC1", "C", ("Z", "h"), "D", "c", 1, ())
        got("YZC1", "C", ("D", "h"), "Z", "c", 1, ())
        if late_route:
            got("Z", "Z", ("own", "h"), "Z", "h", both, (("C", 1), ("Y", 0), ("C", 0)))
            got("C", "C", ("own", "h"), "Y", "c", both, (("Y", 0),))
            got("YZ0", "Y", ("Z", "h"), "D", "h", 0, ())
            got("YC0", "Y", ("Y", "c"), "own", "c", 0, (("Z", 0),))
            got("ZC0", "C", ("Z", "h"), "D", "c", 0, ())
            got("YZC0", "Z", ("own", "c"), "Z", "c", 0, ())
        else:
            got("Z", "Z", ("own", "h"), "Z", "h", both, (("C", 1), ("Y", 0)))
            got("C", "C", ("own", "h"), "Y", "c", both, (("Y", 0), ("Z", 0)))
            got("YZ0", "Y", ("Z", "h"), "D", "h", 0, (("C", 0),))
            got("YC0", "Y", ("Y", "c"), "own", "c", 0, ())
            got("ZC0", "Z", ("Y", "c"), "D", "c", 0, ())
            got("YZC0", "C", ("D", "h"), "Z", "c", 0, ())

        def slot_in(b):
            @task(f"in{j} {b}", waits=heard[b], after=(*here[b], f"g{j} ownT", "locals done"))
            def _():
                pass

        for b in home:
            slot_in(b)
        if j == 0:

            @task("w in", waits=[(("w", b), wb.at[slot[b]]) for b in ("D", "Y", "Z")], after=("w D", "w Y", "w Z", "locals done"))
            def _():
                pass

        def sums(d):
            @task(f"s{j} {d}", after=("w in", *(f"in{j} {b}" for b in home)))
            def _():
                weight = jnp.concatenate([wb[s] for s in range(4)], axis=1)
                r = jnp.concatenate([gg[s, xs[d], :, zz].reshape(256, 384) for s in range(4)], axis=1)
                t = lax.dot_general(r, weight, (((1,), (1,)), ((), ())), preferred_element_type=F32)
                part[xs[d], :, zz] = t.reshape(2, 128, 384)
                if j == 0:
                    net.start(("fz", d), part.at[xs[d], :, zz], fz.at[d], dev["F"])
                elif j != 2:
                    round_x(j, d)

        for d in (2, 1, 3, 0):
            sums(d)

    for j in range(4):
        g_tasks(j)

    def across(d):
        zz = zc[2]

        @task(f"f {d}", waits=[(("fz", d), fz.at[d])], after=("s0 0", f"s2 {d}"))
        def _():
            part[xs[d], :, zz] = part[xs[d], :, zz] + fz[d]
            round_x(2, d)

    for d in (2, 1, 3, 0):
        across(d)

    near = lax.rem(z, 2)

    def gc_mine():
        return pltpu.make_async_copy(gcs.at[near, p], gc_ref.at[:, span("own")], local.at[3])

    def reduce_tasks(j):
        zz = zc[j]
        ready = {3: "f 3", 1: "f 1", 0: "f 0"} if j == 2 else {d: f"s{j} {d}" for d in (3, 1, 0)}
        pieces = HALF if j == 2 else (slice(0, 128),)

        @task(f"r L {j}", waits=[(("r1 L", j), r1.at[j, 0])], after=(ready[3],))
        def _():
            part[xs[3], 0, zz] = part[xs[3], 0, zz] + r1[j, 0]
            for h, rows in enumerate(pieces):
                net.start(("r2 +", j, 0, h), part.at[xs[3], 0, zz, rows], r2.at[j, 0, 0, rows], x_down)

        @task(f"r R {j}", waits=[(("r1 R", j), r1.at[j, 1])], after=(ready[1],))
        def _():
            part[xs[1], 1, zz] = part[xs[1], 1, zz] + r1[j, 1]
            for h, rows in enumerate(pieces):
                net.start(("r2 -", j, 1, h), part.at[xs[1], 1, zz, rows], r2.at[j, 1, 1, rows], x_up)

        waits = [(("r2 +", j, 1), r2.at[j, 0, 1]), (("r2 -", j, 0), r2.at[j, 1, 0])]
        if j == 3:
            waits.append((("qz", 0), qz))

        @task(f"r {j} d", waits=waits, after=(ready[0], *(("r 1 0",) if j == 3 else ())))
        def _():
            pass

        def total(h, rows):
            waits = [(("r2 +", j, 0, h), r2.at[j, 0, 0, rows]), (("r2 -", j, 1, h), r2.at[j, 1, 1, rows])]

            @task(f"r {j} {h}", waits=waits, after=(f"r L {j}", f"r R {j}", f"r {j} d"))
            def _():
                t = part[x, :, zz, rows] + r2[j, 0, :, rows] + r2[j, 1, :, rows]
                if j == 1:
                    part[x, :, zz, rows] = t
                    net.start(("qz", 0), part.at[x, :, zz], qz, dev["F"])
                else:
                    gcs[j - 2, :, rows] = (t if j == 2 else t + qz[:, rows]).astype(BF16)

        for h, rows in enumerate(pieces):
            total(h, rows)

    for j in (1, 2, 3):
        reduce_tasks(j)

    def gc_out(h):
        rows = HALF[h]

        @task(f"gc {h}", after=(f"r 2 {h}", "r 3 0", *(("gc 0",) if h else ())))
        def _():
            to = gc_ref.at[rows, span("own")]
            net.start(("gc", "D", h), gcs.at[1 - near, o, rows], to, dev["D"])
            net.start(("gc", "Y", h), gcs.at[near, o, rows], to, dev["Y"])
            net.start(("gc", "Z", h), gcs.at[1 - near, p, rows], to, dev["Z"])
            if h:
                gc_mine().start()

    for h in range(2):
        gc_out(h)

    rows = {"Y": slice(0, 384), "Z": slice(0, 384), "D": slice(128, 384), "own": slice(0, 512)}

    def products(b, js):
        s = slot[b]
        total = 0.0
        for j in js:
            rhs = gg[s, :, :, zc[j]].reshape(1024, 384)
            total = total + jnp.dot(ct[j, rows[b]], rhs, preferred_element_type=F32)
        return total

    slots = ("Y", "D", "own", "Z")

    def early(j, b):
        @task(f"e{j} {b}", after=(f"in{j} {b}", f"turn {j}", *((f"e{j - 1} {b}",) if j else ())))
        def _():
            at = (slot[b], rows[b])
            t = products(b, (j,))
            gw2[at] = gw2[at] + t if j else t

    for j in range(3):
        for b in slots:
            early(j, b)

    gw_copies = (
        pltpu.make_async_copy(gw2.at[slot["own"], slice(0, 384)], gw_ref.at[span("own")], local.at[4]),
        pltpu.make_async_copy(gw2.at[slot["own"], slice(384, 512)], gw_ref.at[third("D")], local.at[6]),
    )

    def late(b):
        @task(f"late {b}", after=(f"e2 {b}", "turn 3", f"in3 {b}"))
        def _():
            at = (slot[b], rows[b])
            gw2[at] = (gw2[at] + products(b, (3,))) * factor
            if b == "own":
                for copy in gw_copies:
                    copy.start()
            else:
                to = rest("own") if b == "D" else span("own")
                net.start(("gw", b), gw2.at[at], gw_ref.at[to], dev[b])

    for b in slots:
        late(b)

    @task("sent", after=("gc 1", *(f"late {b}" for b in slots)))
    def _():
        net.drain(later=("gc", "gw"))

    @task(
        "end",
        waits=[(("gw", b), gw_ref.at[rest(b) if b == "D" else span(b)]) for b in ("Y", "Z", "D")]
        + [(("gc", b, h), gc_ref.at[HALF[h], span(b)]) for b in ("Y", "Z", "D") for h in range(2)],
        after=("sent",),
    )
    def _():
        for copy in gw_copies:
            copy.wait()
        gc_mine().wait()

    run_tasks(tasks, net)
    net.drain()
    assert len(net.index) <= N_SEMS


def hand_over(gc_ref, gw_ref, gc_out, gw_out, gc_buf, gw_buf, read, written):
    rows = gw_ref.shape[0] // PIECES
    routes = [(gw_ref.at[pl.ds(i * rows, rows)], gw_buf.at[pl.ds(i * rows, rows)], gw_out.at[pl.ds(i * rows, rows)]) for i in range(PIECES)]
    routes.insert(0, (gc_ref, gc_buf, gc_out))
    reads = [pltpu.make_async_copy(a, b, read.at[i]) for i, (a, b, _) in enumerate(routes)]
    writes = [pltpu.make_async_copy(b, c, written.at[i]) for i, (_, b, c) in enumerate(routes)]
    for copy in reads:
        copy.start()
    for r, w in zip(reads, writes):
        r.wait()
        w.start()
    for copy in writes:
        copy.wait()


SCRATCH = (
    ((4, 2, 4, 128, 512), BF16),
    ((4, 512, 1024), BF16),
    ((4, 4, 2, 4, 128, 384), BF16),
    ((4, 384, 384), BF16),
    ((4, 2, 4, 128, 384), F32),
    ((4, 2, 128, 384), F32),
    ((4, 2, 2, 128, 384), F32),
    ((2, 128, 384), F32),
    ((4, 2, 128, 384), F32),
    ((4, 512, 384), F32),
    ((2, 2, 128, 384), BF16),
)


def on_device(context, out_weight, grad_out):
    factor = float(4096) ** (-0.5)
    anywhere = pl.BlockSpec(memory_space=pl.ANY)
    results = pl.pallas_call(
        functools.partial(kernel, factor),
        out_shape=(
            jax.ShapeDtypeStruct((128, 1536), BF16),
            jax.ShapeDtypeStruct((1536, 384), F32),
        ),
        in_specs=[anywhere] * 3,
        out_specs=(anywhere, anywhere),
        scratch_shapes=[
            *(pltpu.VMEM(shape, dtype) for shape, dtype in SCRATCH),
            pltpu.SemaphoreType.DMA((N_SEMS,)),
            pltpu.SemaphoreType.DMA((N_SEMS,)),
            pltpu.SemaphoreType.DMA((7,)),
        ],
        compiler_params=pltpu.CompilerParams(
            collective_id=0, has_side_effects=True, vmem_limit_bytes=60 * 2**20
        ),
        cost_estimate=pl.CostEstimate(flops=9663676416, bytes_accessed=5111808, transcendentals=0),
        name="both_gradients",
    )(context, out_weight, grad_out.reshape(2, 4, 128, 384))
    return pl.pallas_call(
        hand_over,
        out_shape=tuple(jax.ShapeDtypeStruct(r.shape, r.dtype) for r in results),
        in_specs=[anywhere] * 2,
        out_specs=(anywhere, anywhere),
        scratch_shapes=[
            pltpu.VMEM((128, 1536), BF16),
            pltpu.VMEM((1536, 384), F32),
            pltpu.SemaphoreType.DMA((1 + PIECES,)),
            pltpu.SemaphoreType.DMA((1 + PIECES,)),
        ],
        cost_estimate=pl.CostEstimate(flops=0, bytes_accessed=5505024, transcendentals=0),
        name="hand_over",
    )(*results)


def solution(mesh):
    fine = Mesh(mesh.devices.reshape(4, 2, 4, 2, 2), AXES)
    dp, tensor = ("x", "ylo", "z"), ("yhi", "core")
    return jax.shard_map(
        on_device,
        mesh=fine,
        in_specs=(P(dp, tensor), P(tensor, dp), P(tensor, dp)),
        out_specs=(P(dp, tensor), P(tensor, dp)),
        check_vma=False,
    )
```
